128 devices in a mesh: replica: 32 (over x, y, z_lo), fsdp: 4 (over z_hi, core).
Axes of the slice: x: 4, y: 4, z: 4 (z_hi: 2, z_lo: 2; z = z_hi * 2 + z_lo), core: 2. Of those that a mesh axis runs over, the one named last changes fastest.
Arguments:
- deltas: bfloat16 [32, 2048, 5120], P('replica', 'fsdp'), may hold values from -6 to 6
- master: float32 [2048, 5120], P('fsdp', 'replica'), may hold values from -6 to 6
- momentum: float32 [2048, 5120], P('fsdp', 'replica'), may hold values from -3 to 3
- inputs: bfloat16 [32, 2048, 2560], P('replica', 'fsdp'), may hold values from -6 to 6
- inner_weight: bfloat16 [32, 2560, 2560], P('replica', 'fsdp'), may hold values from -0.125 to 0.125
- cotangent: bfloat16 [32, 2048, 2560], P('replica', 'fsdp'), may hold values from -6 to 6
Outputs:
- new_master: float32 [2048, 5120], P('fsdp', 'replica')
- new_momentum: float32 [2048, 5120], P('fsdp', 'replica')
- new_weights: bfloat16 [2048, 5120], P('fsdp')
- input_grad: bfloat16 [32, 2048, 2560], P('replica', 'fsdp')
- weight_grad: bfloat16 [32, 2560, 2560], P('replica', 'fsdp')
The draws below stay inside these ranges and needn't reach their ends.
All inputs are finite; a program needn't handle non-finite values.
Results may differ from the reference program's by a relative error of at most 0.015.
Values may be sent and summed in bfloat16 or wider, within the bound.
A program may use at most 128 MiB of HBM per device.

```python
import jax
import jax.numpy as jnp
from jax import lax

D = 5120
FRAG_ROWS = 2048
DIN = 2560
DOUT = 2560
TOK_DEV = 512
TOK_REP = 2048
REPLICAS = 32
N_FSDP = 4


def spiked(values, rng, source, target, parts, factor):
    def block_of(axis_at):
        return (jnp.arange(values.shape[axis_at]) // (values.shape[axis_at] // parts)).reshape((-1,) + (1,) * (values.ndim - 1 - axis_at))

    first = jax.random.permutation(rng, parts)[block_of(target)]
    second = (block_of(target) + parts // 2) % parts
    return jnp.where((block_of(source) == first) | (block_of(source) == second), factor * values, values)


def levels(stream_key, extent, split, smallest, top_value):
    def one(axis_at, parts):
        draws = jax.random.uniform(jax.random.fold_in(jax.random.fold_in(stream_key, 6), axis_at), (parts,), jnp.float32, smallest / len(split), top_value / len(split))
        return jnp.repeat(jnp.exp(draws), extent[axis_at] // parts).reshape((-1,) + (1,) * (len(extent) - axis_at - 1))

    loudness = one(*split[0])
    for cut in split[1:]:
        loudness = loudness * one(*cut)
    return loudness


def normal_values(rng, shape, scale, bound, shards=(), kind=jnp.bfloat16):
    result = scale * jax.random.normal(rng, shape, jnp.float32)
    if shards:
        result = result * levels(rng, shape, shards, -0.22, 0.18)
    return jnp.clip(result, -bound, bound).astype(kind)


def heavy_noise(own_key, dims, deviation, reach, split, heavy, dtype=jnp.bfloat16):
    array = deviation * jax.random.normal(own_key, dims, jnp.float32)
    if split:
        array = array * levels(own_key, dims, split, -0.22, 0.18)
    return jnp.clip(spiked(array, jax.random.fold_in(own_key, 3), *heavy), -reach, reach).astype(dtype)


def setup_inputs(seed: int = 0) -> dict:
    seeds = jax.random.split(jax.random.key(seed), 7)
    return {
        "deltas": heavy_noise(seeds[0], (REPLICAS, FRAG_ROWS, D), 1.0, 6.0, ((0, 32), (1, 4)), (0, 2, 32, 2.75)),
        "master": normal_values(seeds[1], (FRAG_ROWS, D), 1.0, 6.0, ((0, 4), (1, 32)), jnp.float32),
        "momentum": normal_values(seeds[2], (FRAG_ROWS, D), 0.5, 3.0, ((0, 4), (1, 32)), jnp.float32),
        "inputs": normal_values(seeds[3], (REPLICAS, TOK_REP, DIN), 1.0, 6.0, ((0, 32), (1, 4))),
        "inner_weight": normal_values(seeds[4], (REPLICAS, DIN, DOUT), DIN ** -0.5, 0.125, ((0, 32), (1, 4))),
        "cotangent": normal_values(seeds[5], (REPLICAS, TOK_REP, DOUT), 1.0, 6.0, ((0, 32), (1, 4))),
    }


def inner_replica(operands):
    inputs, weight, cotangent = operands
    input_grad = jnp.dot(cotangent, weight.T, preferred_element_type=jnp.float32).astype(jnp.bfloat16)
    blocks_in = inputs.reshape(N_FSDP, TOK_DEV, DIN).astype(jnp.float32)
    blocks_co = cotangent.reshape(N_FSDP, TOK_DEV, DOUT).astype(jnp.float32)
    partial_sums = jnp.einsum("btk,btn->bkn", blocks_in, blocks_co).astype(jnp.bfloat16)
    weight_grad = jnp.sum(partial_sums.astype(jnp.float32), axis=0).astype(jnp.bfloat16)
    return input_grad, weight_grad


def reference(deltas, master, momentum, inputs, inner_weight, cotangent):
    outer_grad = jnp.sum(deltas.astype(jnp.float32), axis=0) / REPLICAS
    new_momentum = 0.9 * momentum + outer_grad
    new_master = master - 0.7 * (outer_grad + 0.9 * new_momentum)
    new_weights = new_master.astype(jnp.bfloat16)
    input_grad, weight_grad = lax.map(inner_replica, (inputs, inner_weight, cotangent))
    return new_master, new_momentum, new_weights, input_grad, weight_grad
```

```python
import functools

import jax
import jax.numpy as jnp
from jax import lax
from jax.experimental import pallas as pl
from jax.experimental.pallas import tpu as pltpu
from jax.sharding import PartitionSpec as P

MESH = pl.DeviceIdType.MESH
BF16 = jnp.bfloat16
F32 = jnp.float32

ROWS, D = 512, 5120
HALF = ROWS // 2
XC, YC, ZC = D // 4, D // 16, D // 32
TOK, DIN, DOUT, KC = 512, 2560, 2560, 640
FIRST, SECOND = 7, 2
REPLICAS = 32
N_SEMS = 96
N_LOCAL = 32


def ds(start, size):
    return pl.ds(pl.multiple_of(start, size), size)


def kernel(
    deltas, master, momentum, inputs, weight, cotangent,
    o_master, o_momentum, o_weights, o_input_grad, o_weight_grad,
    c_all, i_all, i_t, w_all, d_all, g_all,
    a_in, b_in, b_t, b1, a_t, v_b, a2, b2, u_f, u_b, r3,
    mast, mom, new, new_a, new_ar, new_b, new_br,
    send_sems, recv_sems, local_sems,
):
    r, f = lax.axis_index("replica"), lax.axis_index("fsdp")
    x, y, zl = r // 8, (r // 2) % 4, r % 2
    h, c = f // 2, f % 2

    def replica_at(x_at, y_at, z_at):
        return ((x_at * 4 + y_at) * 2 + z_at, f)

    over_x = [replica_at((x + j) % 4, y, zl) for j in (1, 2, 3)]
    over_y = [replica_at(x, (y + j) % 4, zl) for j in (1, 2, 3)]
    over_z = replica_at(x, y, 1 - zl)
    f_s, f_p, f_q = h * 2 + 1 - c, (1 - h) * 2 + c, (1 - h) * 2 + 1 - c
    sibling, far, diagonal = (r, f_s), (r, f_p), (r, f_q)

    counts = {"remote": 0, "local": 0}
    sent = []
    stored = []

    def remote(src, dst, device):
        i = counts["remote"]
        counts["remote"] += 1
        copy = pltpu.make_async_remote_copy(
            src_ref=src, dst_ref=dst, send_sem=send_sems.at[i], recv_sem=recv_sems.at[i],
            device_id=device, device_id_type=MESH,
        )
        copy.start()
        sent.append(copy)
        return copy

    def local(src, dst):
        i = counts["local"]
        counts["local"] += 1
        copy = pltpu.make_async_copy(src, dst, local_sems.at[i])
        copy.start()
        return copy

    def store(src, dst):
        stored.append(local(src, dst))

    barrier = pltpu.get_barrier_semaphore()
    partners = over_x + over_y + [over_z, sibling, far, diagonal]
    for device in partners:
        pl.semaphore_signal(barrier, inc=1, device_id=device, device_id_type=MESH)
    pl.semaphore_wait(barrier, len(partners))

    far_c, far_i = [], []
    queue = []
    for j in range(8):
        rows = pl.ds(64 * j, 64)
        queue.append((far_c, cotangent.at[0, rows], c_all.at[2, rows], far))
    for j in range(2):
        rows = pl.ds(256 * j, 256)
        for slot, owner, device in ((2, f_p, far), (3, f_q, diagonal)):
            queue.append((far_i, inputs.at[0, rows, ds(owner * KC, KC)], i_all.at[slot, rows], device))

    def send_far(count):
        for _ in range(count):
            kept, src, dst, device = queue.pop(0)
            kept.append(remote(src, dst, device))

    send_far(2)
    load_b = [
        local(deltas.at[0, pl.ds(HALF, HALF), pl.ds(XC * k, XC)], b_in.at[:, pl.ds(XC * k, XC)])
        for k in range(4)
    ]
    a1 = []
    for j in (1, 3, 2):
        there = (x + j) % 4
        a1.append(remote(deltas.at[0, pl.ds(0, HALF), ds(there * XC, XC)], a_in.at[j], over_x[j - 1]))
    send_far(FIRST - 2)
    load_a = local(deltas.at[0, pl.ds(0, HALF), ds(x * XC, XC)], a_in.at[0])
    load_c = local(cotangent.at[0], c_all.at[0])
    load_w = local(weight.at[0], w_all)
    load_i = local(inputs.at[0, :, ds(f * KC, KC)], i_all.at[0])
    load_m = [local(master, mast), local(momentum, mom)]

    b1_in = []
    for k in range(4):
        load_b[k].wait()

        @pl.loop(0, XC // 256)
        def _(n):
            b_t[k, ds(n * 256, 256), :] = b_in[:, ds(XC * k + n * 256, 256)].T

        for j in (1, 3, 2):
            there = (y + j) % 4
            b1_in.append(remote(b_t.at[k, ds(there * YC, YC)], b1.at[j - 1, k], over_y[j - 1]))

    near_c = remote(cotangent.at[0], c_all.at[1], sibling)
    near_i = remote(inputs.at[0, :, ds(f_s * KC, KC)], i_all.at[1], sibling)

    def grad_of(slot):
        @pl.loop(0, 2)
        def _(n):
            rows = ds(n * 256, 256)
            d_all[slot, rows, :] = lax.dot_general(
                c_all[slot, rows, :], w_all[...], (((1,), (1,)), ((), ())),
                preferred_element_type=F32,
            ).astype(BF16)

    def turn(slot):
        @pl.loop(0, KC // 128)
        def _(n):
            i_t[slot, ds(n * 128, 128), :] = i_all[slot, :, ds(n * 128, 128)].T

    mine = ds(f * KC, KC)
    load_c.wait()
    load_w.wait()
    grad_of(0)
    store(d_all.at[0], o_input_grad.at[0, :, mine])
    near_c.wait_recv()
    grad_of(1)
    grads = [remote(d_all.at[1], o_input_grad.at[0, :, mine], sibling)]
    load_i.wait()
    turn(0)
    near_i.wait_recv()
    turn(1)

    load_a.wait()
    for copy in a1:
        copy.wait_recv()

    @pl.loop(0, XC // 128)
    def _(n):
        columns = ds(n * 128, 128)
        total = a_in[0, :, columns].astype(F32)
        for j in (1, 2, 3):
            total += a_in[j, :, columns].astype(F32)
        a_t[columns, :] = total.astype(BF16).T

    a2_in = []
    for j in (1, 3, 2):
        there = (y + j) % 4
        a2_in.append(remote(a_t.at[ds(there * YC, YC)], a2.at[j - 1], over_y[j - 1]))
    for copy in b1_in:
        copy.wait_recv()

    @pl.loop(0, 4)
    def _(k):
        @pl.loop(0, YC // 64)
        def _(n):
            rows = ds(n * 64, 64)
            total = b_t[k, ds(y * YC + n * 64, 64), :].astype(F32)
            for j in range(3):
                total += b1[j, k, rows, :].astype(F32)
            v_b[k, rows, :] = total.astype(BF16)

    b2_in = []
    for j in (1, 3, 2):
        b2_in.append(remote(v_b.at[(x + j) % 4], b2.at[j - 1], over_x[j - 1]))

    for copy in a2_in + b2_in:
        copy.wait_recv()

    @pl.loop(0, YC // 32)
    def _(n):
        rows = ds(n * 32, 32)
        total_a = a_t[ds(y * YC + n * 32, 32), :].astype(F32)
        total_b = v_b[x, rows, :].astype(F32)
        for j in range(3):
            total_a += a2[j, rows, :].astype(F32)
            total_b += b2[j, rows, :].astype(F32)
        u_f[rows, pl.ds(0, HALF)] = total_a
        u_f[rows, pl.ds(HALF, HALF)] = total_b
        u_b[rows, pl.ds(0, HALF)] = total_a.astype(BF16)
        u_b[rows, pl.ds(HALF, HALF)] = total_b.astype(BF16)

    z_in = remote(u_b.at[ds((1 - zl) * ZC, ZC)], r3, over_z)
    send_far(SECOND)
    for copy in load_m:
        copy.wait()
    z_in.wait_recv()

    @pl.loop(0, ZC // 32)
    def _(n):
        rows = ds(n * 32, 32)
        outer_grad = (u_f[ds(zl * ZC + n * 32, 32), :] + r3[rows, :].astype(F32)) / REPLICAS
        new_momentum = 0.9 * mom[rows, :] + outer_grad
        new_master = mast[rows, :] - 0.7 * (outer_grad + 0.9 * new_momentum)
        mom[rows, :] = new_momentum
        mast[rows, :] = new_master
        new[ds(zl * ZC + n * 32, 32), :] = new_master.astype(BF16)

    n_in = remote(new.at[ds(zl * ZC, ZC)], new.at[ds(zl * ZC, ZC)], over_z)
    send_far(len(queue))
    store(mast, o_master)
    store(mom, o_momentum)
    n_in.wait_recv()

    second = []
    here = ds(y * YC, YC)
    for j in (1, 3, 2):
        second.append(remote(new.at[:, pl.ds(0, HALF)], new_a.at[here], over_y[j - 1]))
        second.append(remote(new.at[:, pl.ds(HALF, HALF)], new_b.at[x, here], over_x[j - 1]))

    @pl.loop(0, YC // 32)
    def _(n):
        rows = ds(n * 32, 32)
        new_a[ds(y * YC + n * 32, 32), :] = new[rows, pl.ds(0, HALF)]
        new_b[x, ds(y * YC + n * 32, 32), :] = new[rows, pl.ds(HALF, HALF)]

    forwards = []
    for j in range(4):
        for copy in far_c[2 * j : 2 * j + 2]:
            copy.wait_recv()
        rows = pl.ds(128 * j, 128)
        if j < 3:
            forwards.append(remote(c_all.at[2, rows], c_all.at[3, rows], sibling))
    for copy in second:
        copy.wait_recv()
    first = []
    for j in (1, 3, 2):
        first.append(remote(new_b.at[:, here], new_b.at[:, here], over_y[j - 1]))

    @pl.loop(0, XC // 128)
    def _(n):
        new_ar[:, ds(n * 128, 128)] = new_a[ds(n * 128, 128), :].T

    theirs = o_weights.at[pl.ds(0, HALF), ds(x * XC, XC)]
    for j in (1, 3, 2):
        first.append(remote(new_ar, theirs, over_x[j - 1]))
    store(new_ar, theirs)
    forwards.append(remote(c_all.at[2, pl.ds(384, 128)], c_all.at[3, pl.ds(384, 128)], sibling))

    grad_of(2)
    grads.append(remote(d_all.at[2], o_input_grad.at[0, :, mine], far))
    for copy in forwards:
        copy.wait_recv()
    grad_of(3)
    grads.append(remote(d_all.at[3], o_input_grad.at[0, :, mine], diagonal))

    for copy in far_i[0::2]:
        copy.wait_recv()
    turn(2)
    for copy in far_i[1::2]:
        copy.wait_recv()
    turn(3)

    @pl.loop(0, DOUT // 256)
    def _(n):
        columns = ds(n * 256, 256)
        total = jnp.dot(i_t[0], c_all[0, :, columns], preferred_element_type=F32)
        for slot in (1, 2, 3):
            total += jnp.dot(i_t[slot], c_all[slot, :, columns], preferred_element_type=F32)
        g_all[:, columns] = total.astype(BF16)

    store(g_all, o_weight_grad.at[0])

    for copy in first:
        copy.wait_recv()
    for k in range(4):
        @pl.loop(0, XC // 256)
        def _(n):
            new_br[:, ds(XC * k + n * 256, 256)] = new_b[k, ds(n * 256, 256), :].T

        columns = pl.ds(XC * k, XC)
        store(new_br.at[:, columns], o_weights.at[pl.ds(HALF, HALF), columns])

    for copy in grads:
        copy.wait_recv()
    for copy in sent:
        copy.wait_send()
    for copy in stored:
        copy.wait()


def per_device(deltas, master, momentum, inputs, inner_weight, cotangent):
    shape = jax.ShapeDtypeStruct
    anywhere = pl.BlockSpec(memory_space=pl.ANY)
    vmem = pltpu.VMEM
    outs = pl.pallas_call(
        kernel,
        out_shape=(
            shape((ZC, ROWS), F32),
            shape((ZC, ROWS), F32),
            shape((ROWS, D), BF16),
            shape((1, TOK, DIN), BF16),
            shape((1, KC, DOUT), BF16),
        ),
        in_specs=[anywhere] * 6,
        out_specs=(anywhere,) * 5,
        scratch_shapes=[
            vmem((4, TOK, DOUT), BF16),
            vmem((4, TOK, KC), BF16),
            vmem((4, KC, TOK), BF16),
            vmem((KC, DOUT), BF16),
            vmem((4, TOK, KC), BF16),
            vmem((KC, DOUT), BF16),
            vmem((4, HALF, XC), BF16),
            vmem((HALF, D), BF16),
            vmem((4, XC, HALF), BF16),
            vmem((3, 4, YC, HALF), BF16),
            vmem((XC, HALF), BF16),
            vmem((4, YC, HALF), BF16),
            vmem((3, YC, HALF), BF16),
            vmem((3, YC, HALF), BF16),
            vmem((YC, ROWS), F32),
            vmem((YC, ROWS), BF16),
            vmem((ZC, ROWS), BF16),
            vmem((ZC, ROWS), F32),
            vmem((ZC, ROWS), F32),
            vmem((YC, ROWS), BF16),
            vmem((XC, HALF), BF16),
            vmem((HALF, XC), BF16),
            vmem((4, XC, HALF), BF16),
            vmem((HALF, D), BF16),
            pltpu.SemaphoreType.DMA((N_SEMS,)),
            pltpu.SemaphoreType.DMA((N_SEMS,)),
            pltpu.SemaphoreType.DMA((N_LOCAL,)),
        ],
        compiler_params=pltpu.CompilerParams(
            collective_id=0, has_side_effects=True, vmem_limit_bytes=60 * 1024 * 1024
        ),
        cost_estimate=pl.CostEstimate(
            flops=4 * TOK * DIN * DOUT, bytes_accessed=40 * 1024 * 1024, transcendentals=0
        ),
        name="outer_step_and_projection_grads",
    )(deltas, master.T, momentum.T, inputs, inner_weight, cotangent)
    new_master, new_momentum, new_weights, input_grad, weight_grad = outs
    return (new_master.T, new_momentum.T, new_weights, input_grad, weight_grad)


def solution(mesh):
    return jax.shard_map(
        per_device,
        mesh=mesh,
        in_specs=(
            P("replica", "fsdp", None),
            P("fsdp", "replica"),
            P("fsdp", "replica"),
            P("replica", "fsdp", None),
            P("replica", "fsdp", None),
            P("replica", "fsdp", None),
        ),
        out_specs=(
            P("fsdp", "replica"),
            P("fsdp", "replica"),
            P("fsdp", None),
            P("replica", "fsdp", None),
            P("replica", "fsdp", None),
        ),
        check_vma=False,
    )
```

```python
import functools

import jax
import jax.numpy as jnp
from jax import lax
from jax.experimental import pallas as pl
from jax.experimental.pallas import tpu as pltpu
from jax.sharding import PartitionSpec as P

MESH = pl.DeviceIdType.MESH
BF16 = jnp.bfloat16
F32 = jnp.float32

ROWS, D = 512, 5120
HALF = ROWS // 2
XC, YC, ZC = D // 4, D // 16, D // 32
TOK, DIN, DOUT, KC = 512, 2560, 2560, 640
FIRST, SECOND = 1, 2
REPLICAS = 32
N_SEMS = 96
N_LOCAL = 32


def ds(start, size):
    return pl.ds(pl.multiple_of(start, size), size)


def kernel(
    deltas, master, momentum, inputs, weight, cotangent,
    o_master, o_momentum, o_weights, o_input_grad, o_weight_grad,
    c_all, i_all, i_t, w_all, d_all, g_all,
    a_in, b_in, b_t, b1, a_t, v_b, a2, b2, u_f, u_b, r3,
    mast, mom, new, new_a, new_ar, new_b,
    send_sems, recv_sems, local_sems,
):
    r, f = lax.axis_index("replica"), lax.axis_index("fsdp")
    x, y, zl = r // 8, (r // 2) % 4, r % 2
    h, c = f // 2, f % 2

    def replica_at(x_at, y_at, z_at):
        return ((x_at * 4 + y_at) * 2 + z_at, f)

    over_x = [replica_at((x + j) % 4, y, zl) for j in (1, 2, 3)]
    over_y = [replica_at(x, (y + j) % 4, zl) for j in (1, 2, 3)]
    over_z = replica_at(x, y, 1 - zl)
    f_s, f_p, f_q = h * 2 + 1 - c, (1 - h) * 2 + c, (1 - h) * 2 + 1 - c
    sibling, far, diagonal = (r, f_s), (r, f_p), (r, f_q)

    counts = {"remote": 0, "local": 0}
    sent = []
    stored = []

    def remote(src, dst, device):
        i = counts["remote"]
        counts["remote"] += 1
        copy = pltpu.make_async_remote_copy(
            src_ref=src, dst_ref=dst, send_sem=send_sems.at[i], recv_sem=recv_sems.at[i],
            device_id=device, device_id_type=MESH,
        )
        copy.start()
        sent.append(copy)
        return copy

    def local(src, dst):
        i = counts["local"]
        counts["local"] += 1
        copy = pltpu.make_async_copy(src, dst, local_sems.at[i])
        copy.start()
        return copy

    def store(src, dst):
        stored.append(local(src, dst))

    barrier = pltpu.get_barrier_semaphore()
    partners = over_x + over_y + [over_z, sibling, far, diagonal]
    for device in partners:
        pl.semaphore_signal(barrier, inc=1, device_id=device, device_id_type=MESH)
    pl.semaphore_wait(barrier, len(partners))

    far_c, far_i = [], []
    queue = []
    for start, size in ((0, 448), (448, 64)):
        rows = pl.ds(start, size)
        queue.append((far_c, cotangent.at[0, rows], c_all.at[2, rows], far))
    for start, size in ((0, 256), (256, 256)):
        rows = pl.ds(start, size)
        for slot, owner, device in ((2, f_p, far), (3, f_q, diagonal)):
            queue.append((far_i, inputs.at[0, rows, ds(owner * KC, KC)], i_all.at[slot, rows], device))

    def send_far(count):
        for _ in range(count):
            kept, src, dst, device = queue.pop(0)
            kept.append(remote(src, dst, device))

    send_far(FIRST)
    load_b = [
        local(deltas.at[0, pl.ds(HALF, HALF), pl.ds(XC * k, XC)], b_in.at[:, pl.ds(XC * k, XC)])
        for k in range(4)
    ]
    a1 = []
    for j in (1, 3, 2):
        there = (x + j) % 4
        a1.append(remote(deltas.at[0, pl.ds(0, HALF), ds(there * XC, XC)], a_in.at[j], over_x[j - 1]))
    load_a = local(deltas.at[0, pl.ds(0, HALF), ds(x * XC, XC)], a_in.at[0])
    load_c = local(cotangent.at[0], c_all.at[0])
    load_w = local(weight.at[0], w_all)
    load_i = local(inputs.at[0, :, ds(f * KC, KC)], i_all.at[0])
    load_m = [local(master, mast), local(momentum, mom)]

    b1_in = []
    for k in range(4):
        load_b[k].wait()

        @pl.loop(0, XC // 256)
        def _(n):
            b_t[k, ds(n * 256, 256), :] = b_in[:, ds(XC * k + n * 256, 256)].T

        for j in (1, 3, 2):
            there = (y + j) % 4
            b1_in.append(remote(b_t.at[k, ds(there * YC, YC)], b1.at[j - 1, k], over_y[j - 1]))

    near_c = remote(cotangent.at[0], c_all.at[1], sibling)
    near_i = remote(inputs.at[0, :, ds(f_s * KC, KC)], i_all.at[1], sibling)

    def grad_of(slot):
        @pl.loop(0, 2)
        def _(n):
            rows = ds(n * 256, 256)
            d_all[slot, rows, :] = lax.dot_general(
                c_all[slot, rows, :], w_all[...], (((1,), (1,)), ((), ())),
                preferred_element_type=F32,
            ).astype(BF16)

    def turn(slot):
        @pl.loop(0, KC // 128)
        def _(n):
            i_t[slot, ds(n * 128, 128), :] = i_all[slot, :, ds(n * 128, 128)].T

    mine = ds(f * KC, KC)
    load_c.wait()
    load_w.wait()
    grad_of(0)
    store(d_all.at[0], o_input_grad.at[0, :, mine])
    near_c.wait_recv()
    grad_of(1)
    grads = [remote(d_all.at[1], o_input_grad.at[0, :, mine], sibling)]
    load_i.wait()
    turn(0)
    near_i.wait_recv()
    turn(1)

    load_a.wait()
    for copy in a1:
        copy.wait_recv()

    @pl.loop(0, XC // 128)
    def _(n):
        columns = ds(n * 128, 128)
        total = a_in[0, :, columns].astype(F32)
        for j in (1, 2, 3):
            total += a_in[j, :, columns].astype(F32)
        a_t[columns, :] = total.astype(BF16).T

    a2_in = []
    for j in (1, 3, 2):
        there = (y + j) % 4
        a2_in.append(remote(a_t.at[ds(there * YC, YC)], a2.at[j - 1], over_y[j - 1]))
    for copy in b1_in:
        copy.wait_recv()

    @pl.loop(0, 4)
    def _(k):
        @pl.loop(0, YC // 64)
        def _(n):
            rows = ds(n * 64, 64)
            total = b_t[k, ds(y * YC + n * 64, 64), :].astype(F32)
            for j in range(3):
                total += b1[j, k, rows, :].astype(F32)
            v_b[k, rows, :] = total.astype(BF16)

    b2_in = []
    for j in (1, 3, 2):
        b2_in.append(remote(v_b.at[(x + j) % 4], b2.at[j - 1], over_x[j - 1]))

    for copy in a2_in + b2_in:
        copy.wait_recv()

    @pl.loop(0, YC // 32)
    def _(n):
        rows = ds(n * 32, 32)
        total_a = a_t[ds(y * YC + n * 32, 32), :].astype(F32)
        total_b = v_b[x, rows, :].astype(F32)
        for j in range(3):
            total_a += a2[j, rows, :].astype(F32)
            total_b += b2[j, rows, :].astype(F32)
        u_f[rows, pl.ds(0, HALF)] = total_a
        u_f[rows, pl.ds(HALF, HALF)] = total_b
        u_b[rows, pl.ds(0, HALF)] = total_a.astype(BF16)
        u_b[rows, pl.ds(HALF, HALF)] = total_b.astype(BF16)

    z_in = remote(u_b.at[ds((1 - zl) * ZC, ZC)], r3, over_z)
    send_far(SECOND)
    for copy in load_m:
        copy.wait()
    z_in.wait_recv()

    @pl.loop(0, ZC // 32)
    def _(n):
        rows = ds(n * 32, 32)
        outer_grad = (u_f[ds(zl * ZC + n * 32, 32), :] + r3[rows, :].astype(F32)) / REPLICAS
        new_momentum = 0.9 * mom[rows, :] + outer_grad
        new_master = mast[rows, :] - 0.7 * (outer_grad + 0.9 * new_momentum)
        mom[rows, :] = new_momentum
        mast[rows, :] = new_master
        new[ds(zl * ZC + n * 32, 32), :] = new_master.astype(BF16)

    n_in = remote(new.at[ds(zl * ZC, ZC)], new.at[ds(zl * ZC, ZC)], over_z)
    send_far(len(queue))
    store(mast, o_master)
    store(mom, o_momentum)
    n_in.wait_recv()

    second = []
    here = ds(y * YC, YC)
    for j in (1, 3, 2):
        second.append(remote(new.at[:, pl.ds(0, HALF)], new_a.at[here], over_y[j - 1]))
        second.append(remote(new.at[:, pl.ds(HALF, HALF)], new_b.at[x, here], over_x[j - 1]))

    @pl.loop(0, YC // 32)
    def _(n):
        rows = ds(n * 32, 32)
        new_a[ds(y * YC + n * 32, 32), :] = new[rows, pl.ds(0, HALF)]
        new_b[x, ds(y * YC + n * 32, 32), :] = new[rows, pl.ds(HALF, HALF)]

    forwards = []
    for copy, rows in zip(far_c, (pl.ds(0, 448), pl.ds(448, 64))):
        copy.wait_recv()
        forwards.append(remote(c_all.at[2, rows], c_all.at[3, rows], sibling))
    for copy in second:
        copy.wait_recv()
    first = []
    for j in (1, 3, 2):
        first.append(remote(new_b.at[:, here], new_b.at[:, here], over_y[j - 1]))

    @pl.loop(0, XC // 128)
    def _(n):
        new_ar[:, ds(n * 128, 128)] = new_a[ds(n * 128, 128), :].T

    theirs = o_weights.at[pl.ds(0, HALF), ds(x * XC, XC)]
    for j in (1, 3, 2):
        first.append(remote(new_ar, theirs, over_x[j - 1]))
    store(new_ar, theirs)

    grad_of(2)
    grads.append(remote(d_all.at[2], o_input_grad.at[0, :, mine], far))
    for copy in forwards:
        copy.wait_recv()
    grad_of(3)
    grads.append(remote(d_all.at[3], o_input_grad.at[0, :, mine], diagonal))

    for copy in far_i[0::2]:
        copy.wait_recv()
    turn(2)
    for copy in far_i[1::2]:
        copy.wait_recv()
    turn(3)

    @pl.loop(0, DOUT // 256)
    def _(n):
        columns = ds(n * 256, 256)
        total = jnp.dot(i_t[0], c_all[0, :, columns], preferred_element_type=F32)
        for slot in (1, 2, 3):
            total += jnp.dot(i_t[slot], c_all[slot, :, columns], preferred_element_type=F32)
        g_all[:, columns] = total.astype(BF16)

    store(g_all, o_weight_grad.at[0])

    for copy in first:
        copy.wait_recv()
    for k in range(4):
        @pl.loop(0, XC // 256)
        def _(n):
            b_in[:, ds(XC * k + n * 256, 256)] = new_b[k, ds(n * 256, 256), :].T

        columns = pl.ds(XC * k, XC)
        store(b_in.at[:, columns], o_weights.at[pl.ds(HALF, HALF), columns])

    for copy in grads:
        copy.wait_recv()
    for copy in sent:
        copy.wait_send()
    for copy in stored:
        copy.wait()


def hand_over(*refs):
    copies = [pltpu.make_async_copy(refs[i], refs[5 + i], refs[10].at[i]) for i in (2, 4, 3, 0, 1)]
    for copy in copies:
        copy.start()
    for copy in copies:
        copy.wait()


def per_device(deltas, master, momentum, inputs, inner_weight, cotangent):
    anywhere = pl.BlockSpec(memory_space=pl.ANY)
    vmem = pltpu.VMEM
    outs = pl.pallas_call(
        kernel,
        out_shape=(
            vmem((ZC, ROWS), F32),
            vmem((ZC, ROWS), F32),
            vmem((ROWS, D), BF16),
            vmem((1, TOK, DIN), BF16),
            vmem((1, KC, DOUT), BF16),
        ),
        in_specs=[anywhere] * 6,
        out_specs=(anywhere,) * 5,
        scratch_shapes=[
            vmem((4, TOK, DOUT), BF16),
            vmem((4, TOK, KC), BF16),
            vmem((4, KC, TOK), BF16),
            vmem((KC, DOUT), BF16),
            vmem((4, TOK, KC), BF16),
            vmem((KC, DOUT), BF16),
            vmem((4, HALF, XC), BF16),
            vmem((HALF, D), BF16),
            vmem((4, XC, HALF), BF16),
            vmem((3, 4, YC, HALF), BF16),
            vmem((XC, HALF), BF16),
            vmem((4, YC, HALF), BF16),
            vmem((3, YC, HALF), BF16),
            vmem((3, YC, HALF), BF16),
            vmem((YC, ROWS), F32),
            vmem((YC, ROWS), BF16),
            vmem((ZC, ROWS), BF16),
            vmem((ZC, ROWS), F32),
            vmem((ZC, ROWS), F32),
            vmem((YC, ROWS), BF16),
            vmem((XC, HALF), BF16),
            vmem((HALF, XC), BF16),
            vmem((4, XC, HALF), BF16),
            pltpu.SemaphoreType.DMA((N_SEMS,)),
            pltpu.SemaphoreType.DMA((N_SEMS,)),
            pltpu.SemaphoreType.DMA((N_LOCAL,)),
        ],
        compiler_params=pltpu.CompilerParams(
            collective_id=0, has_side_effects=True, vmem_limit_bytes=46 * 1024 * 1024
        ),
        cost_estimate=pl.CostEstimate(
            flops=4 * TOK * DIN * DOUT, bytes_accessed=40 * 1024 * 1024, transcendentals=0
        ),
        name="outer_step_and_projection_grads",
    )(deltas, master.T, momentum.T, inputs, inner_weight, cotangent)
    new_master, new_momentum, new_weights, input_grad, weight_grad = pl.pallas_call(
        hand_over,
        out_shape=tuple(jax.ShapeDtypeStruct(out.shape, out.dtype) for out in outs),
        in_specs=[anywhere] * 5,
        out_specs=(anywhere,) * 5,
        scratch_shapes=[pltpu.SemaphoreType.DMA((5,))],
        compiler_params=pltpu.CompilerParams(vmem_limit_bytes=1024 * 1024),
        name="hand_over",
    )(*(pltpu.with_memory_space_constraint(out, pltpu.VMEM) for out in outs))
    return (new_master.T, new_momentum.T, new_weights, input_grad, weight_grad)


def solution(mesh):
    return jax.shard_map(
        per_device,
        mesh=mesh,
        in_specs=(
            P("replica", "fsdp", None),
            P("fsdp", "replica"),
            P("fsdp", "replica"),
            P("replica", "fsdp", None),
            P("replica", "fsdp", None),
            P("replica", "fsdp", None),
        ),
        out_specs=(
            P("fsdp", "replica"),
            P("fsdp", "replica"),
            P("fsdp", None),
            P("replica", "fsdp", None),
            P("replica", "fsdp", None),
        ),
        check_vma=False,
    )
```

```python
import functools

import jax
import jax.numpy as jnp
from jax import lax
from jax.experimental import pallas as pl
from jax.experimental.pallas import tpu as pltpu
from jax.sharding import PartitionSpec as P

MESH = pl.DeviceIdType.MESH
BF16 = jnp.bfloat16
F32 = jnp.float32

ROWS, D = 512, 5120
HALF = ROWS // 2
XC, YC, ZC = D // 4, D // 16, D // 32
TOK, DIN, DOUT, KC = 512, 2560, 2560, 640
FIRST, SECOND = 1, 1
REPLICAS = 32
N_SEMS = 96
N_LOCAL = 32


def ds(start, size):
    return pl.ds(pl.multiple_of(start, size), size)


def kernel(
    deltas, master, momentum, inputs, weight, cotangent,
    o_master, o_momentum, o_weights, o_input_grad, o_weight_grad,
    c_all, i_all, i_t, w_all, d_all, g_all,
    a_in, b_in, b_t, b1, a_t, v_b, a2, b2, u_f, u_b, r3,
    mast, mom, new, new_a, new_ar, new_b,
    send_sems, recv_sems, local_sems, far_sem, chip_sem, others_sem,
):
    r, f = lax.axis_index("replica"), lax.axis_index("fsdp")
    x, y, zl = r // 8, (r // 2) % 4, r % 2
    h, c = f // 2, f % 2

    def replica_at(x_at, y_at, z_at):
        return ((x_at * 4 + y_at) * 2 + z_at, f)

    over_x = [replica_at((x + j) % 4, y, zl) for j in (1, 2, 3)]
    over_y = [replica_at(x, (y + j) % 4, zl) for j in (1, 2, 3)]
    over_z = replica_at(x, y, 1 - zl)
    f_s, f_p, f_q = h * 2 + 1 - c, (1 - h) * 2 + c, (1 - h) * 2 + 1 - c
    sibling, far, diagonal = (r, f_s), (r, f_p), (r, f_q)

    counts = {"remote": 0, "local": 0}
    sent = []
    stored = []

    def remote(src, dst, device):
        i = counts["remote"]
        counts["remote"] += 1
        copy = pltpu.make_async_remote_copy(
            src_ref=src, dst_ref=dst, send_sem=send_sems.at[i], recv_sem=recv_sems.at[i],
            device_id=device, device_id_type=MESH,
        )
        copy.start()
        sent.append(copy)
        return copy

    def local(src, dst):
        i = counts["local"]
        counts["local"] += 1
        copy = pltpu.make_async_copy(src, dst, local_sems.at[i])
        copy.start()
        return copy

    def store(src, dst):
        stored.append(local(src, dst))

    barrier = pltpu.get_barrier_semaphore()

    def tell(sem, device):
        pl.semaphore_signal(sem, inc=1, device_id=device, device_id_type=MESH)

    @pl.when(c == 0)
    def _():
        tell(barrier, far)
        pl.semaphore_wait(barrier, 2)
        tell(far_sem, far)

    @pl.when(c == 1)
    def _():
        tell(barrier, sibling)
        pl.semaphore_wait(chip_sem, 1)

    far_c, far_i = [], []
    queue = []
    for start, size in ((0, 448), (448, 64)):
        rows = pl.ds(start, size)
        queue.append((far_c, cotangent.at[0, rows], c_all.at[2, rows], far))
    for start, size in ((0, 256), (256, 256)):
        rows = pl.ds(start, size)
        for slot, owner, device in ((2, f_p, far), (3, f_q, diagonal)):
            queue.append((far_i, inputs.at[0, rows, ds(owner * KC, KC)], i_all.at[slot, rows], device))

    def send_far(count):
        for _ in range(count):
            kept, src, dst, device = queue.pop(0)
            kept.append(remote(src, dst, device))

    send_far(FIRST)

    @pl.when(c == 0)
    def _():
        pl.semaphore_wait(far_sem, 1)
        tell(chip_sem, sibling)

    load_b = [
        local(deltas.at[0, pl.ds(HALF, HALF), pl.ds(XC * k, XC)], b_in.at[:, pl.ds(XC * k, XC)])
        for k in range(4)
    ]
    @pl.when(c == 1)
    def _():
        others = over_x + over_y + [over_z]
        for device in others:
            tell(barrier, device)
        pl.semaphore_wait(barrier, len(others))
        tell(others_sem, sibling)

    @pl.when(c == 0)
    def _():
        pl.semaphore_wait(others_sem, 1)

    a1 = []
    for j in (1, 3, 2):
        there = (x + j) % 4
        a1.append(remote(deltas.at[0, pl.ds(0, HALF), ds(there * XC, XC)], a_in.at[j], over_x[j - 1]))
    load_a = local(deltas.at[0, pl.ds(0, HALF), ds(x * XC, XC)], a_in.at[0])
    load_c = local(cotangent.at[0], c_all.at[0])
    load_w = local(weight.at[0], w_all)
    load_i = local(inputs.at[0, :, ds(f * KC, KC)], i_all.at[0])
    load_m = [local(master, mast), local(momentum, mom)]

    b1_in = []
    for k in range(4):
        load_b[k].wait()

        @pl.loop(0, XC // 256)
        def _(n):
            b_t[k, ds(n * 256, 256), :] = b_in[:, ds(XC * k + n * 256, 256)].T

        for j in (1, 3, 2):
            there = (y + j) % 4
            b1_in.append(remote(b_t.at[k, ds(there * YC, YC)], b1.at[j - 1, k], over_y[j - 1]))

    near_c = remote(cotangent.at[0], c_all.at[1], sibling)
    near_i = remote(inputs.at[0, :, ds(f_s * KC, KC)], i_all.at[1], sibling)

    def grad_of(slot):
        @pl.loop(0, 2)
        def _(n):
            rows = ds(n * 256, 256)
            d_all[slot, rows, :] = lax.dot_general(
                c_all[slot, rows, :], w_all[...], (((1,), (1,)), ((), ())),
                preferred_element_type=F32,
            ).astype(BF16)

    def turn(slot):
        @pl.loop(0, KC // 128)
        def _(n):
            i_t[slot, ds(n * 128, 128), :] = i_all[slot, :, ds(n * 128, 128)].T

    mine = ds(f * KC, KC)
    load_c.wait()
    load_w.wait()
    grad_of(0)
    store(d_all.at[0], o_input_grad.at[0, :, mine])
    near_c.wait_recv()
    grad_of(1)
    grads = [remote(d_all.at[1], o_input_grad.at[0, :, mine], sibling)]
    load_i.wait()
    turn(0)
    near_i.wait_recv()
    turn(1)

    load_a.wait()
    for copy in a1:
        copy.wait_recv()

    @pl.loop(0, XC // 128)
    def _(n):
        columns = ds(n * 128, 128)
        total = a_in[0, :, columns].astype(F32)
        for j in (1, 2, 3):
            total += a_in[j, :, columns].astype(F32)
        a_t[columns, :] = total.astype(BF16).T

    a2_in = []
    for j in (1, 3, 2):
        there = (y + j) % 4
        a2_in.append(remote(a_t.at[ds(there * YC, YC)], a2.at[j - 1], over_y[j - 1]))
    for copy in b1_in:
        copy.wait_recv()

    @pl.loop(0, 4)
    def _(k):
        @pl.loop(0, YC // 64)
        def _(n):
            rows = ds(n * 64, 64)
            total = b_t[k, ds(y * YC + n * 64, 64), :].astype(F32)
            for j in range(3):
                total += b1[j, k, rows, :].astype(F32)
            v_b[k, rows, :] = total.astype(BF16)

    b2_in = []
    for j in (1, 3, 2):
        b2_in.append(remote(v_b.at[(x + j) % 4], b2.at[j - 1], over_x[j - 1]))

    for copy in a2_in + b2_in:
        copy.wait_recv()

    @pl.loop(0, YC // 32)
    def _(n):
        rows = ds(n * 32, 32)
        total_a = a_t[ds(y * YC + n * 32, 32), :].astype(F32)
        total_b = v_b[x, rows, :].astype(F32)
        for j in range(3):
            total_a += a2[j, rows, :].astype(F32)
            total_b += b2[j, rows, :].astype(F32)
        u_f[rows, pl.ds(0, HALF)] = total_a
        u_f[rows, pl.ds(HALF, HALF)] = total_b
        u_b[rows, pl.ds(0, HALF)] = total_a.astype(BF16)
        u_b[rows, pl.ds(HALF, HALF)] = total_b.astype(BF16)

    z_in = remote(u_b.at[ds((1 - zl) * ZC, ZC)], r3, over_z)
    send_far(SECOND)
    for copy in load_m:
        copy.wait()
    z_in.wait_recv()

    @pl.loop(0, ZC // 32)
    def _(n):
        rows = ds(n * 32, 32)
        outer_grad = (u_f[ds(zl * ZC + n * 32, 32), :] + r3[rows, :].astype(F32)) / REPLICAS
        new_momentum = 0.9 * mom[rows, :] + outer_grad
        new_master = mast[rows, :] - 0.7 * (outer_grad + 0.9 * new_momentum)
        mom[rows, :] = new_momentum
        mast[rows, :] = new_master
        new[ds(zl * ZC + n * 32, 32), :] = new_master.astype(BF16)

    n_in = remote(new.at[ds(zl * ZC, ZC)], new.at[ds(zl * ZC, ZC)], over_z)
    send_far(len(queue))
    store(mast, o_master)
    store(mom, o_momentum)
    n_in.wait_recv()

    second = []
    here = ds(y * YC, YC)
    for j in (1, 3, 2):
        second.append(remote(new.at[:, pl.ds(0, HALF)], new_a.at[here], over_y[j - 1]))
        second.append(remote(new.at[:, pl.ds(HALF, HALF)], new_b.at[x, here], over_x[j - 1]))

    @pl.loop(0, YC // 32)
    def _(n):
        rows = ds(n * 32, 32)
        new_a[ds(y * YC + n * 32, 32), :] = new[rows, pl.ds(0, HALF)]
        new_b[x, ds(y * YC + n * 32, 32), :] = new[rows, pl.ds(HALF, HALF)]

    forwards = []
    for copy, rows in zip(far_c, (pl.ds(0, 448), pl.ds(448, 64))):
        copy.wait_recv()
        forwards.append(remote(c_all.at[2, rows], c_all.at[3, rows], sibling))
    for copy in second:
        copy.wait_recv()
    first = []
    for j in (1, 3, 2):
        first.append(remote(new_b.at[:, here], new_b.at[:, here], over_y[j - 1]))

    @pl.loop(0, XC // 128)
    def _(n):
        new_ar[:, ds(n * 128, 128)] = new_a[ds(n * 128, 128), :].T

    theirs = o_weights.at[pl.ds(0, HALF), ds(x * XC, XC)]
    for j in (1, 3, 2):
        first.append(remote(new_ar, theirs, over_x[j - 1]))
    store(new_ar, theirs)

    grad_of(2)
    grads.append(remote(d_all.at[2], o_input_grad.at[0, :, mine], far))
    for copy in forwards:
        copy.wait_recv()
    grad_of(3)
    grads.append(remote(d_all.at[3], o_input_grad.at[0, :, mine], diagonal))

    for copy in far_i[0::2]:
        copy.wait_recv()
    turn(2)
    for copy in far_i[1::2]:
        copy.wait_recv()
    turn(3)

    @pl.loop(0, DOUT // 256)
    def _(n):
        columns = ds(n * 256, 256)
        total = jnp.dot(i_t[0], c_all[0, :, columns], preferred_element_type=F32)
        for slot in (1, 2, 3):
            total += jnp.dot(i_t[slot], c_all[slot, :, columns], preferred_element_type=F32)
        g_all[:, columns] = total.astype(BF16)

    store(g_all, o_weight_grad.at[0])

    for copy in first:
        copy.wait_recv()
    for k in range(4):
        @pl.loop(0, XC // 256)
        def _(n):
            b_in[:, ds(XC * k + n * 256, 256)] = new_b[k, ds(n * 256, 256), :].T

        columns = pl.ds(XC * k, XC)
        store(b_in.at[:, columns], o_weights.at[pl.ds(HALF, HALF), columns])

    for copy in sent[:-2]:
        copy.wait_send()
    for copy in stored:
        copy.wait()
    for copy in grads:
        copy.wait_recv()
    for copy in sent[-2:]:
        copy.wait_send()


def hand_over(*refs):
    copies = [pltpu.make_async_copy(refs[i], refs[5 + i], refs[10].at[i]) for i in (2, 4, 3, 0, 1)]
    for copy in copies:
        copy.start()
    for copy in copies:
        copy.wait()


def per_device(deltas, master, momentum, inputs, inner_weight, cotangent):
    anywhere = pl.BlockSpec(memory_space=pl.ANY)
    vmem = pltpu.VMEM
    outs = pl.pallas_call(
        kernel,
        out_shape=(
            vmem((ZC, ROWS), F32),
            vmem((ZC, ROWS), F32),
            vmem((ROWS, D), BF16),
            vmem((1, TOK, DIN), BF16),
            vmem((1, KC, DOUT), BF16),
        ),
        in_specs=[anywhere] * 6,
        out_specs=(anywhere,) * 5,
        scratch_shapes=[
            vmem((4, TOK, DOUT), BF16),
            vmem((4, TOK, KC), BF16),
            vmem((4, KC, TOK), BF16),
            vmem((KC, DOUT), BF16),
            vmem((4, TOK, KC), BF16),
            vmem((KC, DOUT), BF16),
            vmem((4, HALF, XC), BF16),
            vmem((HALF, D), BF16),
            vmem((4, XC, HALF), BF16),
            vmem((3, 4, YC, HALF), BF16),
            vmem((XC, HALF), BF16),
            vmem((4, YC, HALF), BF16),
            vmem((3, YC, HALF), BF16),
            vmem((3, YC, HALF), BF16),
            vmem((YC, ROWS), F32),
            vmem((YC, ROWS), BF16),
            vmem((ZC, ROWS), BF16),
            vmem((ZC, ROWS), F32),
            vmem((ZC, ROWS), F32),
            vmem((YC, ROWS), BF16),
            vmem((XC, HALF), BF16),
            vmem((HALF, XC), BF16),
            vmem((4, XC, HALF), BF16),
            pltpu.SemaphoreType.DMA((N_SEMS,)),
            pltpu.SemaphoreType.DMA((N_SEMS,)),
            pltpu.SemaphoreType.DMA((N_LOCAL,)),
            pltpu.SemaphoreType.REGULAR,
            pltpu.SemaphoreType.REGULAR,
            pltpu.SemaphoreType.REGULAR,
        ],
        compiler_params=pltpu.CompilerParams(
            collective_id=0, has_side_effects=True, vmem_limit_bytes=46 * 1024 * 1024
        ),
        cost_estimate=pl.CostEstimate(
            flops=4 * TOK * DIN * DOUT, bytes_accessed=40 * 1024 * 1024, transcendentals=0
        ),
        name="outer_step_and_projection_grads",
    )(deltas, master.T, momentum.T, inputs, inner_weight, cotangent)
    new_master, new_momentum, new_weights, input_grad, weight_grad = pl.pallas_call(
        hand_over,
        out_shape=tuple(jax.ShapeDtypeStruct(out.shape, out.dtype) for out in outs),
        in_specs=[anywhere] * 5,
        out_specs=(anywhere,) * 5,
        scratch_shapes=[pltpu.SemaphoreType.DMA((5,))],
        compiler_params=pltpu.CompilerParams(vmem_limit_bytes=1024 * 1024),
        name="hand_over",
    )(*(pltpu.with_memory_space_constraint(out, pltpu.VMEM) for out in outs))
    return (new_master.T, new_momentum.T, new_weights, input_grad, weight_grad)


def solution(mesh):
    return jax.shard_map(
        per_device,
        mesh=mesh,
        in_specs=(
            P("replica", "fsdp", None),
            P("fsdp", "replica"),
            P("fsdp", "replica"),
            P("replica", "fsdp", None),
            P("replica", "fsdp", None),
            P("replica", "fsdp", None),
        ),
        out_specs=(
            P("fsdp", "replica"),
            P("fsdp", "replica"),
            P("fsdp", None),
            P("replica", "fsdp", None),
            P("replica", "fsdp", None),
        ),
        check_vma=False,
    )
```

```python
import functools

import jax
import jax.numpy as jnp
from jax import lax
from jax.experimental import pallas as pl
from jax.experimental.pallas import tpu as pltpu
from jax.sharding import PartitionSpec as P

MESH = pl.DeviceIdType.MESH
BF16 = jnp.bfloat16
F32 = jnp.float32

ROWS, D = 512, 5120
HALF = ROWS // 2
XC, YC, ZC = D // 4, D // 16, D // 32
TOK, DIN, DOUT, KC = 512, 2560, 2560, 640
FIRST, SECOND = 1, 2
REPLICAS = 32
N_SEMS = 96
N_LOCAL = 32


def ds(start, size):
    return pl.ds(pl.multiple_of(start, size), size)


def kernel(
    deltas, master, momentum, inputs, weight, cotangent,
    o_master, o_momentum, o_weights, o_input_grad, o_weight_grad,
    c_all, i_all, i_t, w_all, d_all, g_all,
    a_in, b_in, b_t, b1, a_t, v_b, a2, b2, u_f, u_b, r3,
    mast, mom, new, new_a, new_ar, new_b,
    send_sems, recv_sems, local_sems, far_sem, chip_sem, others_sem,
):
    r, f = lax.axis_index("replica"), lax.axis_index("fsdp")
    x, y, zl = r // 8, (r // 2) % 4, r % 2
    h, c = f // 2, f % 2

    def replica_at(x_at, y_at, z_at):
        return ((x_at * 4 + y_at) * 2 + z_at, f)

    over_x = [replica_at((x + j) % 4, y, zl) for j in (1, 2, 3)]
    over_y = [replica_at(x, (y + j) % 4, zl) for j in (1, 2, 3)]
    over_z = replica_at(x, y, 1 - zl)
    f_s, f_p, f_q = h * 2 + 1 - c, (1 - h) * 2 + c, (1 - h) * 2 + 1 - c
    sibling, far, diagonal = (r, f_s), (r, f_p), (r, f_q)

    counts = {"remote": 0, "local": 0}
    sent = []
    stored = []

    def remote(src, dst, device):
        i = counts["remote"]
        counts["remote"] += 1
        copy = pltpu.make_async_remote_copy(
            src_ref=src, dst_ref=dst, send_sem=send_sems.at[i], recv_sem=recv_sems.at[i],
            device_id=device, device_id_type=MESH,
        )
        copy.start()
        sent.append(copy)
        return copy

    def local(src, dst):
        i = counts["local"]
        counts["local"] += 1
        copy = pltpu.make_async_copy(src, dst, local_sems.at[i])
        copy.start()
        return copy

    def store(src, dst):
        stored.append(local(src, dst))

    barrier = pltpu.get_barrier_semaphore()

    def tell(sem, device):
        pl.semaphore_signal(sem, inc=1, device_id=device, device_id_type=MESH)

    @pl.when(c == 0)
    def _():
        tell(barrier, far)
        pl.semaphore_wait(barrier, 2)
        tell(far_sem, far)

    @pl.when(c == 1)
    def _():
        tell(barrier, sibling)
        pl.semaphore_wait(chip_sem, 1)

    far_c, far_i = [], []
    queue = []
    for start, size in ((0, 480), (480, 32)):
        rows = pl.ds(start, size)
        queue.append((far_c, cotangent.at[0, rows], c_all.at[2, rows], far))
    for start, size in ((0, 256), (256, 256)):
        rows = pl.ds(start, size)
        for slot, owner, device in ((2, f_p, far), (3, f_q, diagonal)):
            queue.append((far_i, inputs.at[0, rows, ds(owner * KC, KC)], i_all.at[slot, rows], device))

    def send_far(count):
        for _ in range(count):
            kept, src, dst, device = queue.pop(0)
            kept.append(remote(src, dst, device))

    send_far(FIRST)

    @pl.when(c == 0)
    def _():
        pl.semaphore_wait(far_sem, 1)
        tell(chip_sem, sibling)

    load_b = [
        local(deltas.at[0, pl.ds(HALF, HALF), pl.ds(XC * k, XC)], b_in.at[:, pl.ds(XC * k, XC)])
        for k in range(4)
    ]
    @pl.when(c == 1)
    def _():
        others = over_x + over_y + [over_z]
        for device in others:
            tell(barrier, device)
        pl.semaphore_wait(barrier, len(others))
        tell(others_sem, sibling)

    @pl.when(c == 0)
    def _():
        pl.semaphore_wait(others_sem, 1)

    a1 = []
    for j in (1, 3, 2):
        there = (x + j) % 4
        a1.append(remote(deltas.at[0, pl.ds(0, HALF), ds(there * XC, XC)], a_in.at[j], over_x[j - 1]))
    load_a = local(deltas.at[0, pl.ds(0, HALF), ds(x * XC, XC)], a_in.at[0])
    load_c = local(cotangent.at[0], c_all.at[0])
    load_w = local(weight.at[0], w_all)
    load_i = local(inputs.at[0, :, ds(f * KC, KC)], i_all.at[0])
    load_m = [local(master, mast), local(momentum, mom)]

    b1_in = []
    for k in range(4):
        load_b[k].wait()

        @pl.loop(0, XC // 256)
        def _(n):
            b_t[k, ds(n * 256, 256), :] = b_in[:, ds(XC * k + n * 256, 256)].T

        for j in (1, 3, 2):
            there = (y + j) % 4
            b1_in.append(remote(b_t.at[k, ds(there * YC, YC)], b1.at[j - 1, k], over_y[j - 1]))

    near_c = remote(cotangent.at[0], c_all.at[1], sibling)
    near_i = remote(inputs.at[0, :, ds(f_s * KC, KC)], i_all.at[1], sibling)

    def grad_of(slot):
        @pl.loop(0, 2)
        def _(n):
            rows = ds(n * 256, 256)
            d_all[slot, rows, :] = lax.dot_general(
                c_all[slot, rows, :], w_all[...], (((1,), (1,)), ((), ())),
                preferred_element_type=F32,
            ).astype(BF16)

    def turn(slot):
        @pl.loop(0, KC // 128)
        def _(n):
            i_t[slot, ds(n * 128, 128), :] = i_all[slot, :, ds(n * 128, 128)].T

    mine = ds(f * KC, KC)
    load_c.wait()
    load_w.wait()
    grad_of(0)
    store(d_all.at[0], o_input_grad.at[0, :, mine])
    near_c.wait_recv()
    grad_of(1)
    grads = [remote(d_all.at[1], o_input_grad.at[0, :, mine], sibling)]
    load_i.wait()
    turn(0)
    near_i.wait_recv()
    turn(1)

    load_a.wait()
    for copy in a1:
        copy.wait_recv()

    @pl.loop(0, XC // 128)
    def _(n):
        columns = ds(n * 128, 128)
        total = a_in[0, :, columns].astype(F32)
        for j in (1, 2, 3):
            total += a_in[j, :, columns].astype(F32)
        a_t[columns, :] = total.astype(BF16).T

    a2_in = []
    for j in (1, 3, 2):
        there = (y + j) % 4
        a2_in.append(remote(a_t.at[ds(there * YC, YC)], a2.at[j - 1], over_y[j - 1]))
    for copy in b1_in:
        copy.wait_recv()

    @pl.loop(0, 4)
    def _(k):
        @pl.loop(0, YC // 64)
        def _(n):
            rows = ds(n * 64, 64)
            total = b_t[k, ds(y * YC + n * 64, 64), :].astype(F32)
            for j in range(3):
                total += b1[j, k, rows, :].astype(F32)
            v_b[k, rows, :] = total.astype(BF16)

    b2_in = []
    for j in (1, 3, 2):
        b2_in.append(remote(v_b.at[(x + j) % 4], b2.at[j - 1], over_x[j - 1]))

    for copy in a2_in + b2_in:
        copy.wait_recv()

    @pl.loop(0, YC // 32)
    def _(n):
        rows = ds(n * 32, 32)
        total_a = a_t[ds(y * YC + n * 32, 32), :].astype(F32)
        total_b = v_b[x, rows, :].astype(F32)
        for j in range(3):
            total_a += a2[j, rows, :].astype(F32)
            total_b += b2[j, rows, :].astype(F32)
        u_f[rows, pl.ds(0, HALF)] = total_a
        u_f[rows, pl.ds(HALF, HALF)] = total_b
        u_b[rows, pl.ds(0, HALF)] = total_a.astype(BF16)
        u_b[rows, pl.ds(HALF, HALF)] = total_b.astype(BF16)

    z_in = remote(u_b.at[ds((1 - zl) * ZC, ZC)], r3, over_z)
    send_far(SECOND)
    for copy in load_m:
        copy.wait()
    z_in.wait_recv()

    @pl.loop(0, ZC // 32)
    def _(n):
        rows = ds(n * 32, 32)
        outer_grad = (u_f[ds(zl * ZC + n * 32, 32), :] + r3[rows, :].astype(F32)) / REPLICAS
        new_momentum = 0.9 * mom[rows, :] + outer_grad
        new_master = mast[rows, :] - 0.7 * (outer_grad + 0.9 * new_momentum)
        mom[rows, :] = new_momentum
        mast[rows, :] = new_master
        new[ds(zl * ZC + n * 32, 32), :] = new_master.astype(BF16)

    n_in = remote(new.at[ds(zl * ZC, ZC)], new.at[ds(zl * ZC, ZC)], over_z)
    send_far(len(queue))
    store(mast, o_master)
    store(mom, o_momentum)
    n_in.wait_recv()

    second = []
    here = ds(y * YC, YC)
    for j in (1, 3, 2):
        second.append(remote(new.at[:, pl.ds(0, HALF)], new_a.at[here], over_y[j - 1]))
        second.append(remote(new.at[:, pl.ds(HALF, HALF)], new_b.at[x, here], over_x[j - 1]))

    @pl.loop(0, YC // 32)
    def _(n):
        rows = ds(n * 32, 32)
        new_a[ds(y * YC + n * 32, 32), :] = new[rows, pl.ds(0, HALF)]
        new_b[x, ds(y * YC + n * 32, 32), :] = new[rows, pl.ds(HALF, HALF)]

    forwards = []
    for copy, rows in zip(far_c, (pl.ds(0, 480), pl.ds(480, 32))):
        copy.wait_recv()
        forwards.append(remote(c_all.at[2, rows], c_all.at[3, rows], sibling))
    for copy in second:
        copy.wait_recv()
    first = []
    for j in (1, 3, 2):
        first.append(remote(new_b.at[:, here], new_b.at[:, here], over_y[j - 1]))

    @pl.loop(0, XC // 128)
    def _(n):
        new_ar[:, ds(n * 128, 128)] = new_a[ds(n * 128, 128), :].T

    theirs = o_weights.at[pl.ds(0, HALF), ds(x * XC, XC)]
    for j in (1, 3, 2):
        first.append(remote(new_ar, theirs, over_x[j - 1]))
    store(new_ar, theirs)

    grad_of(2)
    grads.append(remote(d_all.at[2], o_input_grad.at[0, :, mine], far))
    for copy in forwards:
        copy.wait_recv()
    grad_of(3)
    grads.append(remote(d_all.at[3], o_input_grad.at[0, :, mine], diagonal))

    for copy in far_i[0::2]:
        copy.wait_recv()
    turn(2)
    for copy in far_i[1::2]:
        copy.wait_recv()
    turn(3)

    @pl.loop(0, DOUT // 256)
    def _(n):
        columns = ds(n * 256, 256)
        total = jnp.dot(i_t[0], c_all[0, :, columns], preferred_element_type=F32)
        for slot in (1, 2, 3):
            total += jnp.dot(i_t[slot], c_all[slot, :, columns], preferred_element_type=F32)
        g_all[:, columns] = total.astype(BF16)

    store(g_all, o_weight_grad.at[0])

    for copy in first:
        copy.wait_recv()
    for k in range(4):
        @pl.loop(0, XC // 256)
        def _(n):
            b_in[:, ds(XC * k + n * 256, 256)] = new_b[k, ds(n * 256, 256), :].T

        columns = pl.ds(XC * k, XC)
        store(b_in.at[:, columns], o_weights.at[pl.ds(HALF, HALF), columns])

    for copy in sent[:-2]:
        copy.wait_send()
    for copy in stored:
        copy.wait()
    for copy in grads:
        copy.wait_recv()
    for copy in sent[-2:]:
        copy.wait_send()


def hand_over(*refs):
    copies = [pltpu.make_async_copy(refs[i], refs[5 + i], refs[10].at[i]) for i in (2, 4, 3, 0, 1)]
    for copy in copies:
        copy.start()
    for copy in copies:
        copy.wait()


def per_device(deltas, master, momentum, inputs, inner_weight, cotangent):
    anywhere = pl.BlockSpec(memory_space=pl.ANY)
    vmem = pltpu.VMEM
    outs = pl.pallas_call(
        kernel,
        out_shape=(
            vmem((ZC, ROWS), F32),
            vmem((ZC, ROWS), F32),
            vmem((ROWS, D), BF16),
            vmem((1, TOK, DIN), BF16),
            vmem((1, KC, DOUT), BF16),
        ),
        in_specs=[anywhere] * 6,
        out_specs=(anywhere,) * 5,
        scratch_shapes=[
            vmem((4, TOK, DOUT), BF16),
            vmem((4, TOK, KC), BF16),
            vmem((4, KC, TOK), BF16),
            vmem((KC, DOUT), BF16),
            vmem((4, TOK, KC), BF16),
            vmem((KC, DOUT), BF16),
            vmem((4, HALF, XC), BF16),
            vmem((HALF, D), BF16),
            vmem((4, XC, HALF), BF16),
            vmem((3, 4, YC, HALF), BF16),
            vmem((XC, HALF), BF16),
            vmem((4, YC, HALF), BF16),
            vmem((3, YC, HALF), BF16),
            vmem((3, YC, HALF), BF16),
            vmem((YC, ROWS), F32),
            vmem((YC, ROWS), BF16),
            vmem((ZC, ROWS), BF16),
            vmem((ZC, ROWS), F32),
            vmem((ZC, ROWS), F32),
            vmem((YC, ROWS), BF16),
            vmem((XC, HALF), BF16),
            vmem((HALF, XC), BF16),
            vmem((4, XC, HALF), BF16),
            pltpu.SemaphoreType.DMA((N_SEMS,)),
            pltpu.SemaphoreType.DMA((N_SEMS,)),
            pltpu.SemaphoreType.DMA((N_LOCAL,)),
            pltpu.SemaphoreType.REGULAR,
            pltpu.SemaphoreType.REGULAR,
            pltpu.SemaphoreType.REGULAR,
        ],
        compiler_params=pltpu.CompilerParams(
            collective_id=0, has_side_effects=True, vmem_limit_bytes=46 * 1024 * 1024
        ),
        cost_estimate=pl.CostEstimate(
            flops=4 * TOK * DIN * DOUT, bytes_accessed=40 * 1024 * 1024, transcendentals=0
        ),
        name="outer_step_and_projection_grads",
    )(deltas, master.T, momentum.T, inputs, inner_weight, cotangent)
    new_master, new_momentum, new_weights, input_grad, weight_grad = pl.pallas_call(
        hand_over,
        out_shape=tuple(jax.ShapeDtypeStruct(out.shape, out.dtype) for out in outs),
        in_specs=[anywhere] * 5,
        out_specs=(anywhere,) * 5,
        scratch_shapes=[pltpu.SemaphoreType.DMA((5,))],
        compiler_params=pltpu.CompilerParams(vmem_limit_bytes=1024 * 1024),
        name="hand_over",
    )(*(pltpu.with_memory_space_constraint(out, pltpu.VMEM) for out in outs))
    return (new_master.T, new_momentum.T, new_weights, input_grad, weight_grad)


def solution(mesh):
    return jax.shard_map(
        per_device,
        mesh=mesh,
        in_specs=(
            P("replica", "fsdp", None),
            P("fsdp", "replica"),
            P("fsdp", "replica"),
            P("replica", "fsdp", None),
            P("replica", "fsdp", None),
            P("replica", "fsdp", None),
        ),
        out_specs=(
            P("fsdp", "replica"),
            P("fsdp", "replica"),
            P("fsdp", None),
            P("replica", "fsdp", None),
            P("replica", "fsdp", None),
        ),
        check_vma=False,
    )
```

```python
import functools

import jax
import jax.numpy as jnp
from jax import lax
from jax.experimental import pallas as pl
from jax.experimental.pallas import tpu as pltpu
from jax.sharding import PartitionSpec as P

MESH = pl.DeviceIdType.MESH
BF16 = jnp.bfloat16
F32 = jnp.float32

ROWS, D = 512, 5120
HALF = ROWS // 2
XC, YC, ZC = D // 4, D // 16, D // 32
TOK, DIN, DOUT, KC = 512, 2560, 2560, 640
FIRST, SECOND = 1, 2
REPLICAS = 32
N_SEMS = 31
N_LOCAL = 10


def ds(start, size):
    return pl.ds(pl.multiple_of(start, size), size)


def kernel(
    deltas, master, momentum, inputs, weight, cotangent,
    o_master, o_momentum, o_weights, o_input_grad, o_weight_grad,
    c_all, i_all, i_t, w_all, d_all, g_all,
    a_in, b_in, b_t, b1, a_t, v_b, a2, b2, u_f, u_b, r3,
    mast, mom, new, new_a, new_ar, new_b,
    send_sems, recv_sems, local_sems, far_sem, chip_sem, others_sem,
):
    r, f = lax.axis_index("replica"), lax.axis_index("fsdp")
    x, y, zl = r // 8, (r // 2) % 4, r % 2
    h, c = f // 2, f % 2

    def replica_at(x_at, y_at, z_at):
        return ((x_at * 4 + y_at) * 2 + z_at, f)

    over_x = [replica_at((x + j) % 4, y, zl) for j in (1, 2, 3)]
    over_y = [replica_at(x, (y + j) % 4, zl) for j in (1, 2, 3)]
    over_z = replica_at(x, y, 1 - zl)
    f_s, f_p, f_q = h * 2 + 1 - c, (1 - h) * 2 + c, (1 - h) * 2 + 1 - c
    sibling, far, diagonal = (r, f_s), (r, f_p), (r, f_q)

    counts = {"remote": 0, "local": 0}
    sent = []
    stored = []
    free = []

    def remote(src, dst, device):
        i = counts["remote"]
        counts["remote"] += 1
        copy = pltpu.make_async_remote_copy(
            src_ref=src, dst_ref=dst, send_sem=send_sems.at[i], recv_sem=recv_sems.at[i],
            device_id=device, device_id_type=MESH,
        )
        copy.start()
        sent.append(copy)
        return copy

    def together(whole, pieces):
        i = counts["remote"]
        counts["remote"] += 1
        sems = {"send_sem": send_sems.at[i], "recv_sem": recv_sems.at[i], "device_id_type": MESH}
        for src, dst, device in pieces:
            pltpu.make_async_remote_copy(src_ref=src, dst_ref=dst, device_id=device, **sems).start()
        copy = pltpu.make_async_remote_copy(src_ref=whole, dst_ref=whole, device_id=sibling, **sems)
        sent.append(copy)
        return copy

    def local(src, dst):
        if free:
            i = free.pop()
        else:
            i = counts["local"]
            counts["local"] += 1
        copy = pltpu.make_async_copy(src, dst, local_sems.at[i])
        copy.start()
        return copy, i

    def landed(load):
        load[0].wait()
        free.append(load[1])

    def store(src, dst):
        stored.append(local(src, dst)[0])

    barrier = pltpu.get_barrier_semaphore()

    def tell(sem, device):
        pl.semaphore_signal(sem, inc=1, device_id=device, device_id_type=MESH)

    @pl.when(c == 0)
    def _():
        tell(barrier, far)
        pl.semaphore_wait(barrier, 2)
        tell(far_sem, far)

    @pl.when(c == 1)
    def _():
        tell(barrier, sibling)
        pl.semaphore_wait(chip_sem, 1)

    far_c, far_i = [], []
    queue = []
    for start, size in ((0, 480), (480, 32)):
        rows = pl.ds(start, size)
        queue.append((far_c, cotangent.at[0, rows], c_all.at[2, rows], far))
    for start, size in ((0, 256), (256, 256)):
        rows = pl.ds(start, size)
        for slot, owner, device in ((2, f_p, far), (3, f_q, diagonal)):
            queue.append((far_i, inputs.at[0, rows, ds(owner * KC, KC)], i_all.at[slot, rows], device))

    def send_far(count):
        for _ in range(count):
            kept, src, dst, device = queue.pop(0)
            kept.append(remote(src, dst, device))

    send_far(FIRST)

    @pl.when(c == 0)
    def _():
        pl.semaphore_wait(far_sem, 1)
        tell(chip_sem, sibling)

    load_b = [
        local(deltas.at[0, pl.ds(HALF, HALF), pl.ds(XC * k, XC)], b_in.at[:, pl.ds(XC * k, XC)])
        for k in range(4)
    ]
    @pl.when(c == 1)
    def _():
        others = over_x + over_y + [over_z]
        for device in others:
            tell(barrier, device)
        pl.semaphore_wait(barrier, len(others))
        tell(others_sem, sibling)

    @pl.when(c == 0)
    def _():
        pl.semaphore_wait(others_sem, 1)

    a1_in = together(a_in.at[pl.ds(1, 3)], [
        (deltas.at[0, pl.ds(0, HALF), ds((x + j) % 4 * XC, XC)], a_in.at[j], over_x[j - 1])
        for j in (1, 3, 2)
    ])
    load_a = local(deltas.at[0, pl.ds(0, HALF), ds(x * XC, XC)], a_in.at[0])
    load_c = local(cotangent.at[0], c_all.at[0])
    load_w = local(weight.at[0], w_all)
    load_i = local(inputs.at[0, :, ds(f * KC, KC)], i_all.at[0])
    load_m = [local(master, mast), local(momentum, mom)]

    b1_sems = {"send_sem": send_sems.at[counts["remote"]], "recv_sem": recv_sems.at[counts["remote"]]}
    for k in range(4):
        landed(load_b[k])

        @pl.loop(0, XC // 256)
        def _(n):
            b_t[k, ds(n * 256, 256), :] = b_in[:, ds(XC * k + n * 256, 256)].T

        for j in (1, 3, 2):
            there = (y + j) % 4
            pltpu.make_async_remote_copy(
                src_ref=b_t.at[k, ds(there * YC, YC)], dst_ref=b1.at[j - 1, k],
                device_id=over_y[j - 1], device_id_type=MESH, **b1_sems,
            ).start()
    b1_in = together(b1, [])

    near_c = remote(cotangent.at[0], c_all.at[1], sibling)
    near_i = remote(inputs.at[0, :, ds(f_s * KC, KC)], i_all.at[1], sibling)

    def grad_of(slot):
        @pl.loop(0, 2)
        def _(n):
            rows = ds(n * 256, 256)
            d_all[slot, rows, :] = lax.dot_general(
                c_all[slot, rows, :], w_all[...], (((1,), (1,)), ((), ())),
                preferred_element_type=F32,
            ).astype(BF16)

    def turn(slot):
        @pl.loop(0, KC // 128)
        def _(n):
            i_t[slot, ds(n * 128, 128), :] = i_all[slot, :, ds(n * 128, 128)].T

    mine = ds(f * KC, KC)
    landed(load_c)
    landed(load_w)
    grad_of(0)
    store(d_all.at[0], o_input_grad.at[0, :, mine])
    near_c.wait_recv()
    grad_of(1)
    grads = [remote(d_all.at[1], o_input_grad.at[0, :, mine], sibling)]
    landed(load_i)
    turn(0)
    near_i.wait_recv()
    turn(1)

    landed(load_a)
    a1_in.wait_recv()

    @pl.loop(0, XC // 128)
    def _(n):
        columns = ds(n * 128, 128)
        total = a_in[0, :, columns].astype(F32)
        for j in (1, 2, 3):
            total += a_in[j, :, columns].astype(F32)
        a_t[columns, :] = total.astype(BF16).T

    a2_in = together(a2, [
        (a_t.at[ds((y + j) % 4 * YC, YC)], a2.at[j - 1], over_y[j - 1]) for j in (1, 3, 2)
    ])
    b1_in.wait_recv()

    @pl.loop(0, 4)
    def _(k):
        @pl.loop(0, YC // 64)
        def _(n):
            rows = ds(n * 64, 64)
            total = b_t[k, ds(y * YC + n * 64, 64), :].astype(F32)
            for j in range(3):
                total += b1[j, k, rows, :].astype(F32)
            v_b[k, rows, :] = total.astype(BF16)

    b2_in = together(b2, [(v_b.at[(x + j) % 4], b2.at[j - 1], over_x[j - 1]) for j in (1, 3, 2)])

    a2_in.wait_recv()
    b2_in.wait_recv()

    @pl.loop(0, YC // 32)
    def _(n):
        rows = ds(n * 32, 32)
        total_a = a_t[ds(y * YC + n * 32, 32), :].astype(F32)
        total_b = v_b[x, rows, :].astype(F32)
        for j in range(3):
            total_a += a2[j, rows, :].astype(F32)
            total_b += b2[j, rows, :].astype(F32)
        u_f[rows, pl.ds(0, HALF)] = total_a
        u_f[rows, pl.ds(HALF, HALF)] = total_b
        u_b[rows, pl.ds(0, HALF)] = total_a.astype(BF16)
        u_b[rows, pl.ds(HALF, HALF)] = total_b.astype(BF16)

    z_in = remote(u_b.at[ds((1 - zl) * ZC, ZC)], r3, over_z)
    send_far(SECOND)
    for load in load_m:
        landed(load)
    z_in.wait_recv()

    @pl.loop(0, ZC // 32)
    def _(n):
        rows = ds(n * 32, 32)
        outer_grad = (u_f[ds(zl * ZC + n * 32, 32), :] + r3[rows, :].astype(F32)) / REPLICAS
        new_momentum = 0.9 * mom[rows, :] + outer_grad
        new_master = mast[rows, :] - 0.7 * (outer_grad + 0.9 * new_momentum)
        mom[rows, :] = new_momentum
        mast[rows, :] = new_master
        new[ds(zl * ZC + n * 32, 32), :] = new_master.astype(BF16)

    n_in = remote(new.at[ds(zl * ZC, ZC)], new.at[ds(zl * ZC, ZC)], over_z)
    send_far(len(queue))
    store(mast, o_master)
    store(mom, o_momentum)
    n_in.wait_recv()

    second = []
    here = ds(y * YC, YC)
    for j in (1, 3, 2):
        second.append(remote(new.at[:, pl.ds(0, HALF)], new_a.at[here], over_y[j - 1]))
        second.append(remote(new.at[:, pl.ds(HALF, HALF)], new_b.at[x, here], over_x[j - 1]))

    @pl.loop(0, YC // 32)
    def _(n):
        rows = ds(n * 32, 32)
        new_a[ds(y * YC + n * 32, 32), :] = new[rows, pl.ds(0, HALF)]
        new_b[x, ds(y * YC + n * 32, 32), :] = new[rows, pl.ds(HALF, HALF)]

    forwards = []
    for copy, rows in zip(far_c, (pl.ds(0, 480), pl.ds(480, 32))):
        copy.wait_recv()
        forwards.append(remote(c_all.at[2, rows], c_all.at[3, rows], sibling))
    for copy in second:
        copy.wait_recv()
    first = []
    for j in (1, 3, 2):
        first.append(remote(new_b.at[:, here], new_b.at[:, here], over_y[j - 1]))

    @pl.loop(0, XC // 128)
    def _(n):
        new_ar[:, ds(n * 128, 128)] = new_a[ds(n * 128, 128), :].T

    theirs = o_weights.at[pl.ds(0, HALF), ds(x * XC, XC)]
    for j in (1, 3, 2):
        first.append(remote(new_ar, theirs, over_x[j - 1]))
    store(new_ar, theirs)

    grad_of(2)
    grads.append(remote(d_all.at[2], o_input_grad.at[0, :, mine], far))
    for copy in forwards:
        copy.wait_recv()
    grad_of(3)
    grads.append(remote(d_all.at[3], o_input_grad.at[0, :, mine], diagonal))

    for copy in far_i[0::2]:
        copy.wait_recv()
    turn(2)
    for copy in far_i[1::2]:
        copy.wait_recv()
    turn(3)

    @pl.loop(0, DOUT // 256)
    def _(n):
        columns = ds(n * 256, 256)
        total = jnp.dot(i_t[0], c_all[0, :, columns], preferred_element_type=F32)
        for slot in (1, 2, 3):
            total += jnp.dot(i_t[slot], c_all[slot, :, columns], preferred_element_type=F32)
        g_all[:, columns] = total.astype(BF16)

    store(g_all, o_weight_grad.at[0])

    for copy in first:
        copy.wait_recv()
    for k in range(4):
        @pl.loop(0, XC // 256)
        def _(n):
            b_in[:, ds(XC * k + n * 256, 256)] = new_b[k, ds(n * 256, 256), :].T

        columns = pl.ds(XC * k, XC)
        store(b_in.at[:, columns], o_weights.at[pl.ds(HALF, HALF), columns])

    for copy in sent[:-2]:
        copy.wait_send()
    for copy in stored:
        copy.wait()
    for copy in grads:
        copy.wait_recv()
    for copy in sent[-2:]:
        copy.wait_send()


def hand_over(*refs):
    copies = [pltpu.make_async_copy(refs[i], refs[5 + i], refs[10].at[i]) for i in (2, 4, 3, 0, 1)]
    for copy in copies:
        copy.start()
    for copy in copies:
        copy.wait()


def per_device(deltas, master, momentum, inputs, inner_weight, cotangent):
    anywhere = pl.BlockSpec(memory_space=pl.ANY)
    vmem = pltpu.VMEM
    outs = pl.pallas_call(
        kernel,
        out_shape=(
            vmem((ZC, ROWS), F32),
            vmem((ZC, ROWS), F32),
            vmem((ROWS, D), BF16),
            vmem((1, TOK, DIN), BF16),
            vmem((1, KC, DOUT), BF16),
        ),
        in_specs=[anywhere] * 6,
        out_specs=(anywhere,) * 5,
        scratch_shapes=[
            vmem((4, TOK, DOUT), BF16),
            vmem((4, TOK, KC), BF16),
            vmem((4, KC, TOK), BF16),
            vmem((KC, DOUT), BF16),
            vmem((4, TOK, KC), BF16),
            vmem((KC, DOUT), BF16),
            vmem((4, HALF, XC), BF16),
            vmem((HALF, D), BF16),
            vmem((4, XC, HALF), BF16),
            vmem((3, 4, YC, HALF), BF16),
            vmem((XC, HALF), BF16),
            vmem((4, YC, HALF), BF16),
            vmem((3, YC, HALF), BF16),
            vmem((3, YC, HALF), BF16),
            vmem((YC, ROWS), F32),
            vmem((YC, ROWS), BF16),
            vmem((ZC, ROWS), BF16),
            vmem((ZC, ROWS), F32),
            vmem((ZC, ROWS), F32),
            vmem((YC, ROWS), BF16),
            vmem((XC, HALF), BF16),
            vmem((HALF, XC), BF16),
            vmem((4, XC, HALF), BF16),
            pltpu.SemaphoreType.DMA((N_SEMS,)),
            pltpu.SemaphoreType.DMA((N_SEMS,)),
            pltpu.SemaphoreType.DMA((N_LOCAL,)),
            pltpu.SemaphoreType.REGULAR,
            pltpu.SemaphoreType.REGULAR,
            pltpu.SemaphoreType.REGULAR,
        ],
        compiler_params=pltpu.CompilerParams(
            collective_id=0, has_side_effects=True, vmem_limit_bytes=46 * 1024 * 1024
        ),
        cost_estimate=pl.CostEstimate(
            flops=4 * TOK * DIN * DOUT, bytes_accessed=40 * 1024 * 1024, transcendentals=0
        ),
        name="outer_step_and_projection_grads",
    )(deltas, master.T, momentum.T, inputs, inner_weight, cotangent)
    new_master, new_momentum, new_weights, input_grad, weight_grad = pl.pallas_call(
        hand_over,
        out_shape=tuple(jax.ShapeDtypeStruct(out.shape, out.dtype) for out in outs),
        in_specs=[anywhere] * 5,
        out_specs=(anywhere,) * 5,
        scratch_shapes=[pltpu.SemaphoreType.DMA((5,))],
        compiler_params=pltpu.CompilerParams(vmem_limit_bytes=1024 * 1024),
        name="hand_over",
    )(*(pltpu.with_memory_space_constraint(out, pltpu.VMEM) for out in outs))
    return (new_master.T, new_momentum.T, new_weights, input_grad, weight_grad)


def solution(mesh):
    return jax.shard_map(
        per_device,
        mesh=mesh,
        in_specs=(
            P("replica", "fsdp", None),
            P("fsdp", "replica"),
            P("fsdp", "replica"),
            P("replica", "fsdp", None),
            P("replica", "fsdp", None),
            P("replica", "fsdp", None),
        ),
        out_specs=(
            P("fsdp", "replica"),
            P("fsdp", "replica"),
            P("fsdp", None),
            P("replica", "fsdp", None),
            P("replica", "fsdp", None),
        ),
        check_vma=False,
    )
```

```python
import functools

import jax
import jax.numpy as jnp
from jax import lax
from jax.experimental import pallas as pl
from jax.experimental.pallas import tpu as pltpu
from jax.sharding import PartitionSpec as P

MESH = pl.DeviceIdType.MESH
BF16 = jnp.bfloat16
F32 = jnp.float32

ROWS, D = 512, 5120
HALF = ROWS // 2
XC, YC, ZC = D // 4, D // 16, D // 32
TOK, DIN, DOUT, KC = 512, 2560, 2560, 640
FIRST, SECOND = 1, 1
REPLICAS = 32
N_SEMS = 16
N_LOCAL = 10


def ds(start, size):
    return pl.ds(pl.multiple_of(start, size), size)


def kernel(
    deltas, master, momentum, inputs, weight, cotangent,
    o_master, o_momentum, o_weights, o_input_grad, o_weight_grad,
    c_all, i_all, i_t, w_all, d_all, g_all,
    a_in, b_in, b_t, b1, a_t, v_b, a2, b2, u_f, u_b, r3,
    mast, mom, new, new_a, new_ar, new_b,
    send_sems, recv_sems, local_sems, far_sem, chip_sem, others_sem,
):
    r, f = lax.axis_index("replica"), lax.axis_index("fsdp")
    x, y, zl = r // 8, (r // 2) % 4, r % 2
    h, c = f // 2, f % 2

    def replica_at(x_at, y_at, z_at):
        return ((x_at * 4 + y_at) * 2 + z_at, f)

    over_x = [replica_at((x + j) % 4, y, zl) for j in (1, 2, 3)]
    over_y = [replica_at(x, (y + j) % 4, zl) for j in (1, 2, 3)]
    over_z = replica_at(x, y, 1 - zl)
    f_s, f_p, f_q = h * 2 + 1 - c, (1 - h) * 2 + c, (1 - h) * 2 + 1 - c
    sibling, far, diagonal = (r, f_s), (r, f_p), (r, f_q)

    counts = {"remote": 0, "local": 0}
    sent = []
    stored = []
    free = []

    def remote(src, dst, device):
        i = counts["remote"]
        counts["remote"] += 1
        copy = pltpu.make_async_remote_copy(
            src_ref=src, dst_ref=dst, send_sem=send_sems.at[i], recv_sem=recv_sems.at[i],
            device_id=device, device_id_type=MESH,
        )
        copy.start()
        sent.append(copy)
        return copy

    def together(whole):
        i = counts["remote"]
        counts["remote"] += 1
        sems = {"send_sem": send_sems.at[i], "recv_sem": recv_sems.at[i], "device_id_type": MESH}

        def send(src, dst, device):
            pltpu.make_async_remote_copy(src_ref=src, dst_ref=dst, device_id=device, **sems).start()

        copy = pltpu.make_async_remote_copy(src_ref=whole, dst_ref=whole, device_id=sibling, **sems)
        sent.append(copy)
        return send, copy

    def local(src, dst):
        if free:
            i = free.pop()
        else:
            i = counts["local"]
            counts["local"] += 1
        copy = pltpu.make_async_copy(src, dst, local_sems.at[i])
        copy.start()
        return copy, i

    def landed(load):
        load[0].wait()
        free.append(load[1])

    def store(src, dst):
        stored.append(local(src, dst)[0])

    barrier = pltpu.get_barrier_semaphore()

    def tell(sem, device):
        pl.semaphore_signal(sem, inc=1, device_id=device, device_id_type=MESH)

    @pl.when(c == 0)
    def _():
        tell(barrier, far)
        pl.semaphore_wait(barrier, 2)
        tell(far_sem, far)

    @pl.when(c == 1)
    def _():
        tell(barrier, sibling)
        pl.semaphore_wait(chip_sem, 1)

    send_far_c, far_c = together(c_all.at[2])
    send_far_i, far_i = together(i_all.at[pl.ds(2, 2)])
    queue = []
    for start, size in ((0, 512),):
        rows = pl.ds(start, size)
        queue.append((send_far_c, cotangent.at[0, rows], c_all.at[2, rows], far))
    for start, size in ((0, 256), (256, 256)):
        rows = pl.ds(start, size)
        for slot, owner, device in ((2, f_p, far), (3, f_q, diagonal)):
            queue.append((send_far_i, inputs.at[0, rows, ds(owner * KC, KC)], i_all.at[slot, rows], device))

    def send_far(count):
        for _ in range(count):
            send, src, dst, device = queue.pop(0)
            send(src, dst, device)

    send_far(FIRST)

    @pl.when(c == 0)
    def _():
        pl.semaphore_wait(far_sem, 1)
        tell(chip_sem, sibling)

    load_b = [
        local(deltas.at[0, pl.ds(HALF, HALF), pl.ds(XC * k, XC)], b_in.at[:, pl.ds(XC * k, XC)])
        for k in range(4)
    ]
    @pl.when(c == 1)
    def _():
        others = over_x + over_y + [over_z]
        for device in others:
            tell(barrier, device)
        pl.semaphore_wait(barrier, len(others))
        tell(others_sem, sibling)

    @pl.when(c == 0)
    def _():
        pl.semaphore_wait(others_sem, 1)

    send, a1_in = together(a_in.at[pl.ds(1, 3)])
    for j in (1, 3, 2):
        send(deltas.at[0, pl.ds(0, HALF), ds((x + j) % 4 * XC, XC)], a_in.at[j], over_x[j - 1])
    load_a = local(deltas.at[0, pl.ds(0, HALF), ds(x * XC, XC)], a_in.at[0])
    load_c = local(cotangent.at[0], c_all.at[0])
    load_w = local(weight.at[0], w_all)
    load_i = local(inputs.at[0, :, ds(f * KC, KC)], i_all.at[0])
    load_m = [local(master, mast), local(momentum, mom)]

    send, b1_in = together(b1)
    for k in range(4):
        landed(load_b[k])

        @pl.loop(0, XC // 256)
        def _(n):
            b_t[k, ds(n * 256, 256), :] = b_in[:, ds(XC * k + n * 256, 256)].T

        for j in (1, 3, 2):
            there = (y + j) % 4
            send(b_t.at[k, ds(there * YC, YC)], b1.at[j - 1, k], over_y[j - 1])

    near_c = remote(cotangent.at[0], c_all.at[1], sibling)
    near_i = remote(inputs.at[0, :, ds(f_s * KC, KC)], i_all.at[1], sibling)

    def grad_of(slot):
        @pl.loop(0, 2)
        def _(n):
            rows = ds(n * 256, 256)
            d_all[slot, rows, :] = lax.dot_general(
                c_all[slot, rows, :], w_all[...], (((1,), (1,)), ((), ())),
                preferred_element_type=F32,
            ).astype(BF16)

    def turn(slot):
        @pl.loop(0, KC // 128)
        def _(n):
            i_t[slot, ds(n * 128, 128), :] = i_all[slot, :, ds(n * 128, 128)].T

    mine = ds(f * KC, KC)
    landed(load_c)
    landed(load_w)
    grad_of(0)
    store(d_all.at[0], o_input_grad.at[0, :, mine])
    near_c.wait_recv()
    grad_of(1)
    send_grad, grads = together(d_all.at[pl.ds(1, 3)])
    send_grad(d_all.at[1], o_input_grad.at[0, :, mine], sibling)
    landed(load_i)
    turn(0)
    near_i.wait_recv()
    turn(1)

    landed(load_a)
    a1_in.wait_recv()

    @pl.loop(0, XC // 128)
    def _(n):
        columns = ds(n * 128, 128)
        total = a_in[0, :, columns].astype(F32)
        for j in (1, 2, 3):
            total += a_in[j, :, columns].astype(F32)
        a_t[columns, :] = total.astype(BF16).T

    send, a2_in = together(a2)
    for j in (1, 3, 2):
        send(a_t.at[ds((y + j) % 4 * YC, YC)], a2.at[j - 1], over_y[j - 1])
    b1_in.wait_recv()

    @pl.loop(0, 4)
    def _(k):
        @pl.loop(0, YC // 64)
        def _(n):
            rows = ds(n * 64, 64)
            total = b_t[k, ds(y * YC + n * 64, 64), :].astype(F32)
            for j in range(3):
                total += b1[j, k, rows, :].astype(F32)
            v_b[k, rows, :] = total.astype(BF16)

    send, b2_in = together(b2)
    for j in (1, 3, 2):
        send(v_b.at[(x + j) % 4], b2.at[j - 1], over_x[j - 1])

    a2_in.wait_recv()
    b2_in.wait_recv()

    @pl.loop(0, YC // 32)
    def _(n):
        rows = ds(n * 32, 32)
        total_a = a_t[ds(y * YC + n * 32, 32), :].astype(F32)
        total_b = v_b[x, rows, :].astype(F32)
        for j in range(3):
            total_a += a2[j, rows, :].astype(F32)
            total_b += b2[j, rows, :].astype(F32)
        u_f[rows, pl.ds(0, HALF)] = total_a
        u_f[rows, pl.ds(HALF, HALF)] = total_b
        u_b[rows, pl.ds(0, HALF)] = total_a.astype(BF16)
        u_b[rows, pl.ds(HALF, HALF)] = total_b.astype(BF16)

    z_in = remote(u_b.at[ds((1 - zl) * ZC, ZC)], r3, over_z)
    send_far(SECOND)
    for load in load_m:
        landed(load)
    z_in.wait_recv()

    @pl.loop(0, ZC // 32)
    def _(n):
        rows = ds(n * 32, 32)
        outer_grad = (u_f[ds(zl * ZC + n * 32, 32), :] + r3[rows, :].astype(F32)) / REPLICAS
        new_momentum = 0.9 * mom[rows, :] + outer_grad
        new_master = mast[rows, :] - 0.7 * (outer_grad + 0.9 * new_momentum)
        mom[rows, :] = new_momentum
        mast[rows, :] = new_master
        new[ds(zl * ZC + n * 32, 32), :] = new_master.astype(BF16)

    n_in = remote(new.at[ds(zl * ZC, ZC)], new.at[ds(zl * ZC, ZC)], over_z)
    send_far(len(queue))
    store(mast, o_master)
    store(mom, o_momentum)
    n_in.wait_recv()

    here = ds(y * YC, YC)
    send_a, a2_out = together(a2)
    send_b, b2_out = together(b2)
    for j in (1, 3, 2):
        send_a(new.at[:, pl.ds(0, HALF)], new_a.at[here], over_y[j - 1])
        send_b(new.at[:, pl.ds(HALF, HALF)], new_b.at[x, here], over_x[j - 1])

    @pl.loop(0, YC // 32)
    def _(n):
        rows = ds(n * 32, 32)
        new_a[ds(y * YC + n * 32, 32), :] = new[rows, pl.ds(0, HALF)]
        new_b[x, ds(y * YC + n * 32, 32), :] = new[rows, pl.ds(HALF, HALF)]

    far_c.wait_recv()
    forward = remote(c_all.at[2], c_all.at[3], sibling)
    a2_out.wait_recv()
    b2_out.wait_recv()
    send, b1_out = together(b1)
    for j in (1, 3, 2):
        send(new_b.at[:, here], new_b.at[:, here], over_y[j - 1])

    @pl.loop(0, XC // 128)
    def _(n):
        new_ar[:, ds(n * 128, 128)] = new_a[ds(n * 128, 128), :].T

    theirs = o_weights.at[pl.ds(0, HALF), ds(x * XC, XC)]
    send, a1_out = together(a_in.at[pl.ds(1, 3)])
    for j in (1, 3, 2):
        send(new_ar, theirs, over_x[j - 1])
    store(new_ar, theirs)

    grad_of(2)
    send_grad(d_all.at[2], o_input_grad.at[0, :, mine], far)
    forward.wait_recv()
    grad_of(3)
    send_grad(d_all.at[3], o_input_grad.at[0, :, mine], diagonal)

    far_i.wait_recv()
    turn(2)
    turn(3)

    @pl.loop(0, DOUT // 256)
    def _(n):
        columns = ds(n * 256, 256)
        total = jnp.dot(i_t[0], c_all[0, :, columns], preferred_element_type=F32)
        for slot in (1, 2, 3):
            total += jnp.dot(i_t[slot], c_all[slot, :, columns], preferred_element_type=F32)
        g_all[:, columns] = total.astype(BF16)

    store(g_all, o_weight_grad.at[0])

    b1_out.wait_recv()
    a1_out.wait_recv()
    for k in range(4):
        @pl.loop(0, XC // 256)
        def _(n):
            b_in[:, ds(XC * k + n * 256, 256)] = new_b[k, ds(n * 256, 256), :].T

        columns = pl.ds(XC * k, XC)
        store(b_in.at[:, columns], o_weights.at[pl.ds(HALF, HALF), columns])

    for copy in sent:
        if copy is not grads:
            copy.wait_send()
    for copy in stored:
        copy.wait()
    grads.wait()


def hand_over(*refs):
    copies = [pltpu.make_async_copy(refs[i], refs[5 + i], refs[10].at[i]) for i in (2, 4, 3, 0, 1)]
    for copy in copies:
        copy.start()
    for copy in copies:
        copy.wait()


def per_device(deltas, master, momentum, inputs, inner_weight, cotangent):
    anywhere = pl.BlockSpec(memory_space=pl.ANY)
    vmem = pltpu.VMEM
    outs = pl.pallas_call(
        kernel,
        out_shape=(
            vmem((ZC, ROWS), F32),
            vmem((ZC, ROWS), F32),
            vmem((ROWS, D), BF16),
            vmem((1, TOK, DIN), BF16),
            vmem((1, KC, DOUT), BF16),
        ),
        in_specs=[anywhere] * 6,
        out_specs=(anywhere,) * 5,
        scratch_shapes=[
            vmem((4, TOK, DOUT), BF16),
            vmem((4, TOK, KC), BF16),
            vmem((4, KC, TOK), BF16),
            vmem((KC, DOUT), BF16),
            vmem((4, TOK, KC), BF16),
            vmem((KC, DOUT), BF16),
            vmem((4, HALF, XC), BF16),
            vmem((HALF, D), BF16),
            vmem((4, XC, HALF), BF16),
            vmem((3, 4, YC, HALF), BF16),
            vmem((XC, HALF), BF16),
            vmem((4, YC, HALF), BF16),
            vmem((3, YC, HALF), BF16),
            vmem((3, YC, HALF), BF16),
            vmem((YC, ROWS), F32),
            vmem((YC, ROWS), BF16),
            vmem((ZC, ROWS), BF16),
            vmem((ZC, ROWS), F32),
            vmem((ZC, ROWS), F32),
            vmem((YC, ROWS), BF16),
            vmem((XC, HALF), BF16),
            vmem((HALF, XC), BF16),
            vmem((4, XC, HALF), BF16),
            pltpu.SemaphoreType.DMA((N_SEMS,)),
            pltpu.SemaphoreType.DMA((N_SEMS,)),
            pltpu.SemaphoreType.DMA((N_LOCAL,)),
            pltpu.SemaphoreType.REGULAR,
            pltpu.SemaphoreType.REGULAR,
            pltpu.SemaphoreType.REGULAR,
        ],
        compiler_params=pltpu.CompilerParams(
            collective_id=0, has_side_effects=True, vmem_limit_bytes=46 * 1024 * 1024
        ),
        cost_estimate=pl.CostEstimate(
            flops=4 * TOK * DIN * DOUT, bytes_accessed=40 * 1024 * 1024, transcendentals=0
        ),
        name="outer_step_and_projection_grads",
    )(deltas, master.T, momentum.T, inputs, inner_weight, cotangent)
    new_master, new_momentum, new_weights, input_grad, weight_grad = pl.pallas_call(
        hand_over,
        out_shape=tuple(jax.ShapeDtypeStruct(out.shape, out.dtype) for out in outs),
        in_specs=[anywhere] * 5,
        out_specs=(anywhere,) * 5,
        scratch_shapes=[pltpu.SemaphoreType.DMA((5,))],
        compiler_params=pltpu.CompilerParams(vmem_limit_bytes=1024 * 1024),
        name="hand_over",
    )(*(pltpu.with_memory_space_constraint(out, pltpu.VMEM) for out in outs))
    return (new_master.T, new_momentum.T, new_weights, input_grad, weight_grad)


def solution(mesh):
    return jax.shard_map(
        per_device,
        mesh=mesh,
        in_specs=(
            P("replica", "fsdp", None),
            P("fsdp", "replica"),
            P("fsdp", "replica"),
            P("replica", "fsdp", None),
            P("replica", "fsdp", None),
            P("replica", "fsdp", None),
        ),
        out_specs=(
            P("fsdp", "replica"),
            P("fsdp", "replica"),
            P("fsdp", None),
            P("replica", "fsdp", None),
            P("replica", "fsdp", None),
        ),
        check_vma=False,
    )
```

```python
import functools

import jax
import jax.numpy as jnp
from jax import lax
from jax.experimental import pallas as pl
from jax.experimental.pallas import tpu as pltpu
from jax.sharding import PartitionSpec as P

MESH = pl.DeviceIdType.MESH
BF16 = jnp.bfloat16
F32 = jnp.float32

ROWS, D = 512, 5120
HALF = ROWS // 2
XC, YC, ZC = D // 4, D // 16, D // 32
TOK, DIN, DOUT, KC = 512, 2560, 2560, 640
FIRST, SECOND = 1, 1
REPLICAS = 32
N_SEMS = 14
N_LOCAL = 10


def ds(start, size):
    return pl.ds(pl.multiple_of(start, size), size)


def kernel(
    deltas, master, momentum, inputs, weight, cotangent,
    o_master, o_momentum, o_weights, o_input_grad, o_weight_grad,
    c_all, i_all, i_t, w_all, d_all, g_all,
    a_in, b_in, b_t, b1, a_t, v_b, a2, b2, u_f, u_b, r3,
    mast, mom, new, new_a, new_ar, new_b,
    send_sems, recv_sems, local_sems, far_sem, chip_sem, others_sem,
):
    r, f = lax.axis_index("replica"), lax.axis_index("fsdp")
    x, y, zl = r // 8, (r // 2) % 4, r % 2
    h, c = f // 2, f % 2

    def replica_at(x_at, y_at, z_at):
        return ((x_at * 4 + y_at) * 2 + z_at, f)

    over_x = [replica_at((x + j) % 4, y, zl) for j in (1, 2, 3)]
    over_y = [replica_at(x, (y + j) % 4, zl) for j in (1, 2, 3)]
    over_z = replica_at(x, y, 1 - zl)
    f_s, f_p, f_q = h * 2 + 1 - c, (1 - h) * 2 + c, (1 - h) * 2 + 1 - c
    sibling, far, diagonal = (r, f_s), (r, f_p), (r, f_q)

    counts = {"remote": 0, "local": 0}
    sent = []
    stored = []
    free = []

    def remote(src, dst, device):
        i = counts["remote"]
        counts["remote"] += 1
        copy = pltpu.make_async_remote_copy(
            src_ref=src, dst_ref=dst, send_sem=send_sems.at[i], recv_sem=recv_sems.at[i],
            device_id=device, device_id_type=MESH,
        )
        copy.start()
        sent.append(copy)
        return copy

    def together(whole):
        i = counts["remote"]
        counts["remote"] += 1
        sems = {"send_sem": send_sems.at[i], "recv_sem": recv_sems.at[i], "device_id_type": MESH}

        def send(src, dst, device):
            pltpu.make_async_remote_copy(src_ref=src, dst_ref=dst, device_id=device, **sems).start()

        copy = pltpu.make_async_remote_copy(src_ref=whole, dst_ref=whole, device_id=sibling, **sems)
        sent.append(copy)
        return send, copy

    def local(src, dst):
        if free:
            i = free.pop()
        else:
            i = counts["local"]
            counts["local"] += 1
        copy = pltpu.make_async_copy(src, dst, local_sems.at[i])
        copy.start()
        return copy, i

    def landed(load):
        load[0].wait()
        free.append(load[1])

    def store(src, dst):
        stored.append(local(src, dst)[0])

    barrier = pltpu.get_barrier_semaphore()

    def tell(sem, device):
        pl.semaphore_signal(sem, inc=1, device_id=device, device_id_type=MESH)

    @pl.when(c == 0)
    def _():
        tell(barrier, far)
        pl.semaphore_wait(barrier, 2)
        tell(far_sem, far)

    @pl.when(c == 1)
    def _():
        tell(barrier, sibling)
        pl.semaphore_wait(chip_sem, 1)

    send_far_c, far_c = together(c_all.at[2])
    send_far_i, far_i = together(i_all.at[pl.ds(2, 2)])
    queue = []
    for start, size in ((0, 512),):
        rows = pl.ds(start, size)
        queue.append((send_far_c, cotangent.at[0, rows], c_all.at[2, rows], far))
    for slot, owner, device, start, size in (
        (2, f_p, far, 0, 256), (2, f_p, far, 256, 256), (3, f_q, diagonal, 0, TOK)
    ):
        rows = pl.ds(start, size)
        queue.append((send_far_i, inputs.at[0, rows, ds(owner * KC, KC)], i_all.at[slot, rows], device))

    def send_far(count):
        for _ in range(count):
            send, src, dst, device = queue.pop(0)
            send(src, dst, device)

    send_far(FIRST)

    @pl.when(c == 0)
    def _():
        pl.semaphore_wait(far_sem, 1)
        tell(chip_sem, sibling)

    load_b = [
        local(deltas.at[0, pl.ds(HALF, HALF), pl.ds(XC * k, XC)], b_in.at[:, pl.ds(XC * k, XC)])
        for k in range(4)
    ]
    @pl.when(c == 1)
    def _():
        others = over_x + over_y + [over_z]
        for device in others:
            tell(barrier, device)
        pl.semaphore_wait(barrier, len(others))
        tell(others_sem, sibling)

    @pl.when(c == 0)
    def _():
        pl.semaphore_wait(others_sem, 1)

    send, a1_in = together(a_in.at[pl.ds(1, 3)])
    for j in (1, 3, 2):
        send(deltas.at[0, pl.ds(0, HALF), ds((x + j) % 4 * XC, XC)], a_in.at[j], over_x[j - 1])
    load_a = local(deltas.at[0, pl.ds(0, HALF), ds(x * XC, XC)], a_in.at[0])
    load_c = local(cotangent.at[0], c_all.at[0])
    load_w = local(weight.at[0], w_all)
    load_i = local(inputs.at[0, :, ds(f * KC, KC)], i_all.at[0])
    load_m = [local(master, mast), local(momentum, mom)]

    send, b1_in = together(b1)
    for k in range(4):
        landed(load_b[k])

        @pl.loop(0, XC // 256)
        def _(n):
            b_t[k, ds(n * 256, 256), :] = b_in[:, ds(XC * k + n * 256, 256)].T

        for j in (1, 3, 2):
            there = (y + j) % 4
            send(b_t.at[k, ds(there * YC, YC)], b1.at[j - 1, k], over_y[j - 1])

    near_c = remote(cotangent.at[0], c_all.at[1], sibling)
    near_i = remote(inputs.at[0, :, ds(f_s * KC, KC)], i_all.at[1], sibling)

    def grad_of(slot):
        @pl.loop(0, 2)
        def _(n):
            rows = ds(n * 256, 256)
            d_all[slot, rows, :] = lax.dot_general(
                c_all[slot, rows, :], w_all[...], (((1,), (1,)), ((), ())),
                preferred_element_type=F32,
            ).astype(BF16)

    def turn(slot):
        @pl.loop(0, KC // 128)
        def _(n):
            i_t[slot, ds(n * 128, 128), :] = i_all[slot, :, ds(n * 128, 128)].T

    mine = ds(f * KC, KC)
    landed(load_c)
    landed(load_w)
    grad_of(0)
    store(d_all.at[0], o_input_grad.at[0, :, mine])
    near_c.wait_recv()
    grad_of(1)
    send_grad, grads = together(d_all.at[pl.ds(1, 3)])
    send_grad(d_all.at[1], o_input_grad.at[0, :, mine], sibling)
    landed(load_i)
    turn(0)
    near_i.wait_recv()
    turn(1)

    landed(load_a)
    a1_in.wait_recv()

    @pl.loop(0, XC // 128)
    def _(n):
        columns = ds(n * 128, 128)
        total = a_in[0, :, columns].astype(F32)
        for j in (1, 2, 3):
            total += a_in[j, :, columns].astype(F32)
        a_t[columns, :] = total.astype(BF16).T

    both = b1.at[pl.ds(0, 2), pl.ds(0, 3)]
    send_second, second_in = together(both)
    for j in (1, 3, 2):
        send_second(a_t.at[ds((y + j) % 4 * YC, YC)], a2.at[j - 1], over_y[j - 1])
    b1_in.wait_recv()

    @pl.loop(0, 4)
    def _(k):
        @pl.loop(0, YC // 64)
        def _(n):
            rows = ds(n * 64, 64)
            total = b_t[k, ds(y * YC + n * 64, 64), :].astype(F32)
            for j in range(3):
                total += b1[j, k, rows, :].astype(F32)
            v_b[k, rows, :] = total.astype(BF16)

    for j in (1, 3, 2):
        send_second(v_b.at[(x + j) % 4], b2.at[j - 1], over_x[j - 1])

    second_in.wait_recv()

    @pl.loop(0, YC // 32)
    def _(n):
        rows = ds(n * 32, 32)
        total_a = a_t[ds(y * YC + n * 32, 32), :].astype(F32)
        total_b = v_b[x, rows, :].astype(F32)
        for j in range(3):
            total_a += a2[j, rows, :].astype(F32)
            total_b += b2[j, rows, :].astype(F32)
        u_f[rows, pl.ds(0, HALF)] = total_a
        u_f[rows, pl.ds(HALF, HALF)] = total_b
        u_b[rows, pl.ds(0, HALF)] = total_a.astype(BF16)
        u_b[rows, pl.ds(HALF, HALF)] = total_b.astype(BF16)

    z_in = remote(u_b.at[ds((1 - zl) * ZC, ZC)], r3, over_z)
    send_far(SECOND)
    for load in load_m:
        landed(load)
    z_in.wait_recv()

    @pl.loop(0, ZC // 32)
    def _(n):
        rows = ds(n * 32, 32)
        outer_grad = (u_f[ds(zl * ZC + n * 32, 32), :] + r3[rows, :].astype(F32)) / REPLICAS
        new_momentum = 0.9 * mom[rows, :] + outer_grad
        new_master = mast[rows, :] - 0.7 * (outer_grad + 0.9 * new_momentum)
        mom[rows, :] = new_momentum
        mast[rows, :] = new_master
        new[ds(zl * ZC + n * 32, 32), :] = new_master.astype(BF16)

    n_in = remote(new.at[ds(zl * ZC, ZC)], new.at[ds(zl * ZC, ZC)], over_z)
    send_far(len(queue))
    store(mast, o_master)
    store(mom, o_momentum)
    n_in.wait_recv()

    here = ds(y * YC, YC)
    send, second_out = together(both)
    for j in (1, 3, 2):
        send(new.at[:, pl.ds(0, HALF)], new_a.at[here], over_y[j - 1])
        send(new.at[:, pl.ds(HALF, HALF)], new_b.at[x, here], over_x[j - 1])

    @pl.loop(0, YC // 32)
    def _(n):
        rows = ds(n * 32, 32)
        new_a[ds(y * YC + n * 32, 32), :] = new[rows, pl.ds(0, HALF)]
        new_b[x, ds(y * YC + n * 32, 32), :] = new[rows, pl.ds(HALF, HALF)]

    far_c.wait_recv()
    forward = remote(c_all.at[2], c_all.at[3], sibling)
    second_out.wait_recv()
    send, b1_out = together(b1)
    for j in (1, 3, 2):
        send(new_b.at[:, here], new_b.at[:, here], over_y[j - 1])

    @pl.loop(0, XC // 128)
    def _(n):
        new_ar[:, ds(n * 128, 128)] = new_a[ds(n * 128, 128), :].T

    theirs = o_weights.at[pl.ds(0, HALF), ds(x * XC, XC)]
    send, a1_out = together(a_in.at[pl.ds(1, 3)])
    for j in (1, 3, 2):
        send(new_ar, theirs, over_x[j - 1])
    store(new_ar, theirs)

    grad_of(2)
    send_grad(d_all.at[2], o_input_grad.at[0, :, mine], far)
    forward.wait_recv()
    grad_of(3)
    send_grad(d_all.at[3], o_input_grad.at[0, :, mine], diagonal)

    far_i.wait_recv()
    turn(2)
    turn(3)

    @pl.loop(0, DOUT // 256)
    def _(n):
        columns = ds(n * 256, 256)
        total = jnp.dot(i_t[0], c_all[0, :, columns], preferred_element_type=F32)
        for slot in (1, 2, 3):
            total += jnp.dot(i_t[slot], c_all[slot, :, columns], preferred_element_type=F32)
        g_all[:, columns] = total.astype(BF16)

    store(g_all, o_weight_grad.at[0])

    b1_out.wait_recv()
    a1_out.wait_recv()
    for k in range(4):
        @pl.loop(0, XC // 256)
        def _(n):
            b_in[:, ds(XC * k + n * 256, 256)] = new_b[k, ds(n * 256, 256), :].T

        columns = pl.ds(XC * k, XC)
        store(b_in.at[:, columns], o_weights.at[pl.ds(HALF, HALF), columns])

    for copy in sent:
        if copy is not grads:
            copy.wait_send()
    for copy in stored:
        copy.wait()
    grads.wait()


def hand_over(*refs):
    copies = [pltpu.make_async_copy(refs[i], refs[5 + i], refs[10].at[i]) for i in (2, 4, 3, 0, 1)]
    for copy in copies:
        copy.start()
    for copy in copies:
        copy.wait()


def per_device(deltas, master, momentum, inputs, inner_weight, cotangent):
    anywhere = pl.BlockSpec(memory_space=pl.ANY)
    vmem = pltpu.VMEM
    outs = pl.pallas_call(
        kernel,
        out_shape=(
            vmem((ZC, ROWS), F32),
            vmem((ZC, ROWS), F32),
            vmem((ROWS, D), BF16),
            vmem((1, TOK, DIN), BF16),
            vmem((1, KC, DOUT), BF16),
        ),
        in_specs=[anywhere] * 6,
        out_specs=(anywhere,) * 5,
        scratch_shapes=[
            vmem((4, TOK, DOUT), BF16),
            vmem((4, TOK, KC), BF16),
            vmem((4, KC, TOK), BF16),
            vmem((KC, DOUT), BF16),
            vmem((4, TOK, KC), BF16),
            vmem((KC, DOUT), BF16),
            vmem((4, HALF, XC), BF16),
            vmem((HALF, D), BF16),
            vmem((4, XC, HALF), BF16),
            vmem((3, 4, YC, HALF), BF16),
            vmem((XC, HALF), BF16),
            vmem((4, YC, HALF), BF16),
            vmem((3, YC, HALF), BF16),
            vmem((3, YC, HALF), BF16),
            vmem((YC, ROWS), F32),
            vmem((YC, ROWS), BF16),
            vmem((ZC, ROWS), BF16),
            vmem((ZC, ROWS), F32),
            vmem((ZC, ROWS), F32),
            vmem((YC, ROWS), BF16),
            vmem((XC, HALF), BF16),
            vmem((HALF, XC), BF16),
            vmem((4, XC, HALF), BF16),
            pltpu.SemaphoreType.DMA((N_SEMS,)),
            pltpu.SemaphoreType.DMA((N_SEMS,)),
            pltpu.SemaphoreType.DMA((N_LOCAL,)),
            pltpu.SemaphoreType.REGULAR,
            pltpu.SemaphoreType.REGULAR,
            pltpu.SemaphoreType.REGULAR,
        ],
        compiler_params=pltpu.CompilerParams(
            collective_id=0, has_side_effects=True, vmem_limit_bytes=46 * 1024 * 1024
        ),
        cost_estimate=pl.CostEstimate(
            flops=4 * TOK * DIN * DOUT, bytes_accessed=40 * 1024 * 1024, transcendentals=0
        ),
        name="outer_step_and_projection_grads",
    )(deltas, master.T, momentum.T, inputs, inner_weight, cotangent)
    new_master, new_momentum, new_weights, input_grad, weight_grad = pl.pallas_call(
        hand_over,
        out_shape=tuple(jax.ShapeDtypeStruct(out.shape, out.dtype) for out in outs),
        in_specs=[anywhere] * 5,
        out_specs=(anywhere,) * 5,
        scratch_shapes=[pltpu.SemaphoreType.DMA((5,))],
        compiler_params=pltpu.CompilerParams(vmem_limit_bytes=1024 * 1024),
        name="hand_over",
    )(*(pltpu.with_memory_space_constraint(out, pltpu.VMEM) for out in outs))
    return (new_master.T, new_momentum.T, new_weights, input_grad, weight_grad)


def solution(mesh):
    return jax.shard_map(
        per_device,
        mesh=mesh,
        in_specs=(
            P("replica", "fsdp", None),
            P("fsdp", "replica"),
            P("fsdp", "replica"),
            P("replica", "fsdp", None),
            P("replica", "fsdp", None),
            P("replica", "fsdp", None),
        ),
        out_specs=(
            P("fsdp", "replica"),
            P("fsdp", "replica"),
            P("fsdp", None),
            P("replica", "fsdp", None),
            P("replica", "fsdp", None),
        ),
        check_vma=False,
    )
```
